32 devices in a mesh: section: 2 (over y), row: 4 (over x, core), col: 4 (over z).
Axes of the slice: x: 2, y: 2, z: 4, core: 2. Of those that a mesh axis runs over, the one named last changes fastest.
Arguments:
- hidden_in: bfloat16 [2, 128, 8192], P('section', 'col', 'row'), may hold values from -600 to 600
- norm_gain: float32 [2, 8192], P('section', 'row'), may hold values from 0.1 to 1.9
- q_weight: bfloat16 [2, 8192, 8192], P('section', 'row', 'col'), may hold values from -0.0625 to 0.0625
- kv_weight: bfloat16 [2, 8192, 2048], P('section', 'row', 'col'), may hold values from -0.0625 to 0.0625
- kv_cache: bfloat16 [2, 8, 1024, 2, 1024], P('section', 'col', 'row'), may hold values from -110 to 110
- lengths: int32 [2, 8], P('section', 'col'), may hold values from 768 to 1024, as said below
Outputs:
- handed: bfloat16 [2, 128, 8192], P('section', 'col', 'row')
- new_kv: bfloat16 [2, 128, 2048], P('section', 'col')
The draws below stay inside these ranges and needn't reach their ends.
Inputs may be any that keep to these rules, and one draw needn't show every extreme that they name: `lengths`: in every section some prompt uses exactly 1024 positions.
All inputs are finite; a program needn't handle non-finite values.
Results may differ from the reference program's by a relative error of at most 0.023.
Values may be sent and summed in bfloat16 or wider, within the bound.
A program may use at most 64 MiB of HBM per device.

```python
import jax
import jax.numpy as jnp
from jax import lax

D = 8192
HEADS = 64
KV_HEADS = 8
HEAD_DIM = 128
SAMPLES = 16
PROMPTS = 8
ROWS = 128
CACHE = 1024
N_SECTION = 2


def draw_hidden_in(key, part):
    key_base, key_rows = jax.random.split(key)
    column = jnp.arange(D, dtype=jnp.float32) / (D - 1)
    row_scale = jnp.power(10.0, jax.random.uniform(key_rows, (N_SECTION, ROWS, 1), jnp.float32))
    base = jnp.clip(jax.random.normal(key_base, (N_SECTION, ROWS, D), jnp.float32), -6.0, 6.0)
    column_scale = jnp.power(10.0, column)
    return (base * row_scale * column_scale[None, None, :]).astype(jnp.bfloat16)


def draw_kv_cache(key, part):
    key_base = jax.random.fold_in(key, 0)
    shape_full = (N_SECTION, PROMPTS, CACHE, 2, KV_HEADS * HEAD_DIM)
    base = jnp.clip(jax.random.normal(key_base, shape_full, jnp.float32), -6.0, 6.0)
    return base.astype(jnp.bfloat16)


def draw_lengths(key, part):
    key_lengths, key_top = jax.random.split(key)
    drawn = jax.random.randint(key_lengths, (N_SECTION, PROMPTS), 3 * CACHE // 4, CACHE + 1)
    chosen = jax.random.randint(key_top, (N_SECTION, 1), 0, PROMPTS)
    places = jnp.arange(PROMPTS, dtype=jnp.int32)[None, :]
    return jnp.where(places == chosen, CACHE, drawn).astype(jnp.int32)


def block_scale(stream_key, shape, shards, least, high):
    level, own = 1.0, jax.random.fold_in(stream_key, 6)
    for position, parts in shards:
        heights = jnp.exp(jax.random.uniform(jax.random.fold_in(own, position), (parts,), jnp.float32, least / len(shards), high / len(shards)))
        level = level * jnp.repeat(heights, shape[position] // parts).reshape([-1 if axis == position else 1 for axis in range(len(shape))])
    return level


def normal_values(own_key, shape, scale, limit, pieces=(), kind=jnp.bfloat16):
    level = block_scale(own_key, shape, pieces, -0.22, 0.18) if pieces else 1.0
    array = jax.random.normal(own_key, shape, jnp.float32) * scale * level
    return jnp.minimum(jnp.maximum(array, -limit), limit).astype(kind)


def setup_inputs(seed: int = 0) -> dict:
    splits = jax.random.split(jax.random.key(seed), 7)
    hidden_in = draw_hidden_in(jax.random.fold_in(splits[6], 71), 0)
    norm_gain = jnp.clip(1.0 + 0.18 * jax.random.normal(splits[1], (N_SECTION, D), jnp.float32), 0.1, 1.9)
    q_weight = normal_values(splits[2], (N_SECTION, D, HEADS * HEAD_DIM), D ** -0.5, 0.0625, ((0, 2), (1, 4), (2, 4)))
    kv_weight = normal_values(splits[3], (N_SECTION, D, 2 * KV_HEADS * HEAD_DIM), D ** -0.5, 0.0625, ((0, 2), (1, 4), (2, 4)))
    kv_cache = draw_kv_cache(jax.random.fold_in(splits[6], 71), 0)
    lengths = draw_lengths(jax.random.fold_in(splits[6], 71), 0)
    return {"hidden_in": hidden_in, "norm_gain": norm_gain, "q_weight": q_weight, "kv_weight": kv_weight, "kv_cache": kv_cache, "lengths": lengths}


EPSILON = 1e-05
FLOOR = -1e+30

def attend(query_heads, cache_keys, cache_values, length, new_keys, new_values):
    score_scale = HEAD_DIM ** (-0.5)
    scores = jnp.einsum('sghd,tgd->sght', query_heads.astype(jnp.float32), cache_keys.astype(jnp.float32)) * score_scale
    own_score = jnp.einsum('sghd,sgd->sgh', query_heads.astype(jnp.float32), new_keys.astype(jnp.float32)) * score_scale
    in_range = jnp.arange(CACHE, dtype=jnp.int32) < length
    top_score = jnp.maximum(lax.optimization_barrier(jnp.max(jnp.where(in_range, scores, FLOOR), axis=-1)), own_score)
    weights = jnp.where(in_range, jnp.exp(scores - top_score[..., None]), 0.0)
    own_weight = jnp.exp(own_score - top_score)
    total_weight = lax.optimization_barrier(jnp.sum(weights, axis=-1)) + own_weight
    rounded = lax.optimization_barrier(weights.astype(jnp.bfloat16)).astype(jnp.float32)
    own_rounded = lax.optimization_barrier(own_weight.astype(jnp.bfloat16)).astype(jnp.float32)
    numerator = jnp.einsum('sght,tgd->sghd', rounded, cache_values.astype(jnp.float32))
    numerator = numerator + own_rounded[..., None] * new_values.astype(jnp.float32)[:, :, None, :]
    return (numerator / total_weight[..., None]).astype(jnp.bfloat16)

def layer_step(hidden, gain, query_weight, pair_weight, cache_block, prompt_lengths):
    widened = hidden.astype(jnp.float32)
    mean_square = lax.optimization_barrier(jnp.mean(widened * widened, axis=-1))
    normed = (widened * lax.rsqrt(mean_square + EPSILON)[:, None] * gain[None, :]).astype(jnp.bfloat16)
    query = jnp.dot(normed, query_weight, preferred_element_type=jnp.float32).astype(jnp.bfloat16)
    new_kv = jnp.dot(normed, pair_weight, preferred_element_type=jnp.float32).astype(jnp.bfloat16)
    prompt_count = prompt_lengths.shape[0]
    group_size = HEADS // KV_HEADS
    query_heads = query.reshape(prompt_count, SAMPLES, KV_HEADS, group_size, HEAD_DIM)
    new_keys = new_kv[:, :KV_HEADS * HEAD_DIM].reshape(prompt_count, SAMPLES, KV_HEADS, HEAD_DIM)
    new_values = new_kv[:, KV_HEADS * HEAD_DIM:].reshape(prompt_count, SAMPLES, KV_HEADS, HEAD_DIM)
    cache_keys = cache_block[:, :, 0].reshape(prompt_count, CACHE, KV_HEADS, HEAD_DIM)
    cache_values = cache_block[:, :, 1].reshape(prompt_count, CACHE, KV_HEADS, HEAD_DIM)
    attended = lax.map(lambda items: attend(*items), (query_heads, cache_keys, cache_values, prompt_lengths, new_keys, new_values))
    return (attended.reshape(prompt_count * SAMPLES, HEADS * HEAD_DIM), new_kv)

def reference(hidden_in, norm_gain, q_weight, kv_weight, kv_cache, lengths):
    attended, new_kv = lax.map(lambda items: layer_step(*items), (hidden_in, norm_gain, q_weight, kv_weight, kv_cache, lengths))
    handed = jnp.roll(attended, 1, axis=0)
    return (handed, new_kv)
```

```python
import functools

import jax
import jax.numpy as jnp
from jax import lax
from jax.experimental import pallas as pl
from jax.experimental.pallas import tpu as pltpu
from jax.sharding import PartitionSpec as P

HEAD_DIM = 128
EPSILON = 1e-05
FLOOR = -1e30
TILE = 512
MESH = pl.DeviceIdType.MESH
F32 = jnp.float32
BF16 = jnp.bfloat16


def kernel(
    dims,
    hidden_ref,
    gain_ref,
    qw_ref,
    kvw_ref,
    cache_ref,
    len_ref,
    handed_ref,
    newkv_ref,
    weights,
    cache,
    gathered,
    parts,
    arrived,
    summed,
    full,
    outs,
    outs_in,
    stat_tile,
    stat_rows,
    stat_in,
    squares,
    final,
    weight_sem,
    cache_sem,
    gather_send,
    gather_recv,
    own_send,
    sum_send,
    sum_recv,
    turn_send,
    turn_recv,
    full_send,
    full_recv,
    out_send,
    out_recv,
    stat_send,
    stat_recv,
    square_send,
    square_recv,
    hand_send,
    hand_recv,
):
    n_sec, n_row, n_col, units, quarter, heads_per, pairs_per, kv_heads = dims
    sec, row, col = lax.axis_index("section"), lax.axis_index("row"), lax.axis_index("col")
    rows, width = hidden_ref.shape
    prompts, slots = cache_ref.shape[0], cache_ref.shape[1]
    samples = rows // prompts
    group = (heads_per * n_col) // kv_heads
    tall = group * samples
    mine = kv_heads // n_row
    q_tiles = qw_ref.shape[1] // TILE
    tiles = units * HEAD_DIM // TILE
    pair_cols = kvw_ref.shape[1]

    def peer(d):
        return lax.rem(row + d, n_row)

    loads = []
    for t in range(q_tiles):
        loads.append(
            pltpu.make_async_copy(
                qw_ref.at[:, pl.ds(t * TILE, TILE)], weights.at[t], weight_sem.at[t]
            )
        )
    for t in range(q_tiles, tiles):
        first = (t - q_tiles) * TILE
        wide = min(TILE, pair_cols - first)
        if wide > 0:
            loads.append(
                pltpu.make_async_copy(
                    kvw_ref.at[:, pl.ds(first, wide)],
                    weights.at[t, :, pl.ds(0, wide)],
                    weight_sem.at[t],
                )
            )
        else:
            loads.append(None)
    for load in loads:
        if load is not None:
            load.start()
    cache_load = pltpu.make_async_copy(cache_ref, cache, cache_sem)
    cache_load.start()

    barrier = pltpu.get_barrier_semaphore()
    for d in range(1, n_row):
        pl.semaphore_signal(barrier, inc=1, device_id=(sec, peer(d), col), device_id_type=MESH)
    for d in range(1, n_col):
        pl.semaphore_signal(
            barrier, inc=1, device_id=(sec, row, lax.rem(col + d, n_col)), device_id_type=MESH
        )
    pl.semaphore_signal(
        barrier, inc=1, device_id=(lax.rem(sec + n_sec - 1, n_sec), row, col), device_id_type=MESH
    )

    for t in range(q_tiles, tiles):
        first = (t - q_tiles) * TILE
        wide = max(0, min(TILE, pair_cols - first))
        if wide < TILE:
            weights[t, :, wide:] = jnp.zeros((width, TILE - wide), BF16)
    widened = hidden_ref[...].astype(F32)
    gathered[col] = (widened * gain_ref[...]).astype(BF16)
    squares[row] = jnp.broadcast_to(
        jnp.sum(widened * widened, axis=1, keepdims=True), (rows, HEAD_DIM)
    )

    pl.semaphore_wait(barrier, n_row - 1 + n_col - 1 + 1)

    def gather_copy(block, to, send_sem):
        return pltpu.make_async_remote_copy(
            src_ref=gathered.at[block],
            dst_ref=gathered.at[block],
            send_sem=send_sem,
            recv_sem=gather_recv.at[block],
            device_id=(sec, row, to),
            device_id_type=MESH,
        )

    below, above = jnp.maximum(col - 1, 0), jnp.minimum(col + 1, n_col - 1)

    @pl.when(col > 0)
    def _():
        gather_copy(col, below, gather_send.at[col]).start()

    @pl.when(col < n_col - 1)
    def _():
        gather_copy(col, above, own_send).start()

    def square_copy(d):
        return pltpu.make_async_remote_copy(
            src_ref=squares.at[row],
            dst_ref=squares.at[row],
            send_sem=square_send.at[d],
            recv_sem=square_recv.at[row],
            device_id=(sec, peer(d), col),
            device_id_type=MESH,
        )

    for d in range(1, n_row):
        square_copy(d).start()

    shorter = jnp.minimum(col, n_col - 1 - col)
    upward = col < n_col - 1 - col

    def block_at(k):
        half = (k + 1) // 2
        near = jnp.where(k % 2 == 1, col + half, col - half)
        far = jnp.where(upward, col + (k - shorter), col - (k - shorter))
        return jnp.where(k <= 2 * shorter, near, far)

    def sum_copy(block, d):
        other = peer(d)
        return pltpu.make_async_remote_copy(
            src_ref=parts.at[block, pl.ds(other * quarter, quarter)],
            dst_ref=arrived.at[block, row],
            send_sem=sum_send.at[block, d],
            recv_sem=sum_recv.at[block, row],
            device_id=(sec, other, col),
            device_id_type=MESH,
        )

    def sum_wait(block, d):
        other = peer(d)
        pltpu.make_async_remote_copy(
            src_ref=arrived.at[block, other],
            dst_ref=arrived.at[block, other],
            send_sem=sum_send.at[block, d],
            recv_sem=sum_recv.at[block, other],
            device_id=(sec, other, col),
            device_id_type=MESH,
        ).wait_recv()

    def full_part(source, part):
        return full.at[pl.ds(source * units + part * quarter, quarter)]

    def full_copy(source, d):
        return pltpu.make_async_remote_copy(
            src_ref=full_part(source, row),
            dst_ref=full_part(source, row),
            send_sem=full_send.at[source, d],
            recv_sem=full_recv.at[source, row],
            device_id=(sec, peer(d), col),
            device_id_type=MESH,
        )

    def turn_copy(block):
        return pltpu.make_async_remote_copy(
            src_ref=summed.at[block],
            dst_ref=full_part(col, row),
            send_sem=turn_send.at[block],
            recv_sem=turn_recv.at[col],
            device_id=(sec, row, block),
            device_id_type=MESH,
        )

    def reduce_block(block):
        total = parts[block, pl.ds(row * quarter, quarter)].astype(F32)
        for d in range(1, n_row):
            sum_wait(block, d)
            total = total + arrived[block, peer(d)].astype(F32)
        total = total.astype(BF16)

        @pl.when(block == col)
        def _():
            full[pl.ds(col * units + row * quarter, quarter)] = total
            for d in range(1, n_row):
                full_copy(col, d).start()

        @pl.when(block != col)
        def _():
            summed[block] = total
            turn_copy(block).start()

    def step(k, carry):
        block = block_at(k)

        @pl.when(k > 0)
        def _():
            gather_copy(block, below, gather_send.at[block]).wait_recv()

        @pl.when(jnp.logical_and(block > col, col > 0))
        def _():
            gather_copy(block, below, gather_send.at[block]).start()

        @pl.when(jnp.logical_and(block < col, col < n_col - 1))
        def _():
            gather_copy(block, above, gather_send.at[block]).start()

        for t in range(tiles):
            if loads[t] is not None:

                @pl.when(k == 0)
                def _():
                    loads[t].wait()

            product = jnp.dot(gathered[block], weights[t], preferred_element_type=F32)
            product = product.astype(BF16)
            for u in range(TILE // HEAD_DIM):
                parts[block, t * (TILE // HEAD_DIM) + u] = product[
                    :, u * HEAD_DIM : (u + 1) * HEAD_DIM
                ]
        for d in range(1, n_row):
            sum_copy(block, d).start()

        @pl.when(k > 0)
        def _():
            reduce_block(block_at(k - 1))

        return carry

    lax.fori_loop(0, n_col, step, 0)
    reduce_block(block_at(n_col - 1))

    def forward(k, carry):
        source = block_at(k)
        pltpu.make_async_remote_copy(
            src_ref=full_part(source, row),
            dst_ref=full_part(source, row),
            send_sem=turn_send.at[source],
            recv_sem=turn_recv.at[source],
            device_id=(sec, row, source),
            device_id_type=MESH,
        ).wait_recv()
        for d in range(1, n_row):
            full_copy(source, d).start()
        return carry

    lax.fori_loop(1, n_col, forward, 0)

    for d in range(1, n_row):
        other = peer(d)
        pltpu.make_async_remote_copy(
            src_ref=squares.at[other],
            dst_ref=squares.at[other],
            send_sem=square_send.at[d],
            recv_sem=square_recv.at[other],
            device_id=(sec, other, col),
            device_id_type=MESH,
        ).wait_recv()
    square_sum = squares[0]
    for i in range(1, n_row):
        square_sum = square_sum + squares[i]
    scaling = lax.rsqrt(square_sum / (width * n_row) + EPSILON)
    cache_load.wait()

    def head_unit(head):
        return (head // heads_per) * units + head % heads_per

    def pair_unit(pair):
        return (pair // pairs_per) * units + heads_per + pair % pairs_per

    def scaled(unit, p):
        some = pl.ds(p * samples, samples)
        factor = scaling[p * samples : (p + 1) * samples]
        return (full[unit, some, :].astype(F32) * factor).astype(BF16)

    def queries(g, p):
        return jnp.concatenate([scaled(head_unit(g * group + i), p) for i in range(group)], axis=0)

    score_scale = HEAD_DIM ** (-0.5)
    lane = lax.broadcasted_iota(jnp.int32, (tall, HEAD_DIM), 1)
    spot = lax.broadcasted_iota(jnp.int32, (1, slots), 1)
    position = row * (slots // 2) + spot // 2
    is_key = spot % 2 == 0

    def attend(g, p):
        q = queries(g, p)
        both = cache[p, :, pl.ds(pl.multiple_of(g * HEAD_DIM, HEAD_DIM), HEAD_DIM)]
        scores = (
            lax.dot_general(q, both, (((1,), (1,)), ((), ())), preferred_element_type=F32)
            * score_scale
        )
        valid = jnp.logical_and(is_key, position < len_ref[0, p])
        scores = jnp.where(valid, scores, FLOOR)
        top = jnp.max(scores, axis=1, keepdims=True)
        weight = jnp.where(valid, jnp.exp(scores - top), 0.0)
        total = jnp.sum(weight, axis=1, keepdims=True)
        moved = pltpu.roll(weight, 1, 1).astype(BF16)
        out = jnp.dot(moved, both, preferred_element_type=F32)
        outs[g, p] = out.astype(BF16)
        at = (g * prompts + p) * 2
        tile = jnp.where(lane == at, top, stat_tile[...])
        stat_tile[...] = jnp.where(lane == at + 1, total, tile)

    def out_copy(dest):
        return pltpu.make_async_remote_copy(
            src_ref=outs.at[pl.ds(dest * mine, mine)],
            dst_ref=outs_in.at[row],
            send_sem=out_send.at[dest],
            recv_sem=out_recv.at[row],
            device_id=(sec, dest, col),
            device_id_type=MESH,
        )

    chunk_heads = max(1, heads_per // group)
    chunk_cols = max(1, group // heads_per)
    chunks = kv_heads // chunk_heads
    stat_tile[...] = jnp.zeros_like(stat_tile)

    def chunk(k, carry):
        j = block_at(k) if chunk_cols == 1 and chunks == n_col else k
        for i in range(chunk_cols):
            source = j * chunk_cols + i
            for d in range(1, n_row):
                other = peer(d)
                pltpu.make_async_remote_copy(
                    src_ref=full_part(source, other),
                    dst_ref=full_part(source, other),
                    send_sem=full_send.at[source, d],
                    recv_sem=full_recv.at[source, other],
                    device_id=(sec, other, col),
                    device_id_type=MESH,
                ).wait_recv()
        for i in range(chunk_heads):
            g = j * chunk_heads + i
            for p in range(prompts):
                attend(g, p)
            dest = g // mine

            @pl.when(jnp.logical_and(g % mine == mine - 1, dest != row))
            def _():
                out_copy(dest).start()

        return carry

    lax.fori_loop(0, chunks, chunk, 0)

    stat_rows[...] = stat_tile[...].T
    per_dest = mine * prompts * 2

    def stat_copy(d):
        other = peer(d)
        return pltpu.make_async_remote_copy(
            src_ref=stat_rows.at[pl.ds(pl.multiple_of(other * per_dest, per_dest), per_dest)],
            dst_ref=stat_in.at[pl.ds(pl.multiple_of(row * per_dest, per_dest), per_dest)],
            send_sem=stat_send.at[d],
            recv_sem=stat_recv.at[row],
            device_id=(sec, other, col),
            device_id_type=MESH,
        )

    for d in range(1, n_row):
        stat_copy(d).start()

    stat_in[n_row * per_dest :] = jnp.zeros((HEAD_DIM - n_row * per_dest, tall), F32)
    here = pl.ds(pl.multiple_of(row * per_dest, per_dest), per_dest)
    stat_in[here] = stat_rows[here]
    outs_in[row] = outs[pl.ds(row * mine, mine)]

    for pair in range(2 * kv_heads):
        newkv_ref[:, pair * HEAD_DIM : (pair + 1) * HEAD_DIM] = (
            full[pair_unit(pair)].astype(F32) * scaling
        ).astype(BF16)

    for d in range(1, n_row):
        other = peer(d)
        landed = pl.ds(pl.multiple_of(other * per_dest, per_dest), per_dest)
        pltpu.make_async_remote_copy(
            src_ref=stat_in.at[landed],
            dst_ref=stat_in.at[landed],
            send_sem=stat_send.at[d],
            recv_sem=stat_recv.at[other],
            device_id=(sec, other, col),
            device_id_type=MESH,
        ).wait_recv()
        pltpu.make_async_remote_copy(
            src_ref=outs_in.at[other],
            dst_ref=outs_in.at[other],
            send_sem=out_send.at[other],
            recv_sem=out_recv.at[other],
            device_id=(sec, other, col),
            device_id_type=MESH,
        ).wait_recv()

    stats = stat_in[...].T
    for i in range(mine):
        g = row * mine + i
        for p in range(prompts):
            q = queries(g, p).astype(F32)
            new_key = jnp.concatenate([scaled(pair_unit(g), p)] * group, axis=0)
            new_value = jnp.concatenate([scaled(pair_unit(kv_heads + g), p)] * group, axis=0)
            own = jnp.sum(q * new_key.astype(F32), axis=1, keepdims=True) * score_scale
            top = own
            tops, totals = [], []
            for s in range(n_row):
                at = s * per_dest + (i * prompts + p) * 2
                tops.append(stats[:, at : at + 1])
                totals.append(stats[:, at + 1 : at + 2])
                top = jnp.maximum(top, tops[-1])
            own_weight = jnp.exp(own - top)
            total = own_weight
            value = own_weight.astype(BF16).astype(F32) * new_value.astype(F32)
            for s in range(n_row):
                keep = jnp.exp(tops[s] - top)
                total = total + keep * totals[s]
                value = value + keep * outs_in[s, i, p].astype(F32)
            done = (value / total).astype(BF16)
            for h in range(group):
                first = (i * group + h) * HEAD_DIM
                final[p * samples : (p + 1) * samples, first : first + HEAD_DIM] = done[
                    h * samples : (h + 1) * samples
                ]

    hand = pltpu.make_async_remote_copy(
        src_ref=final,
        dst_ref=handed_ref,
        send_sem=hand_send,
        recv_sem=hand_recv,
        device_id=(lax.rem(sec + 1, n_sec), row, col),
        device_id_type=MESH,
    )
    hand.start()

    @pl.when(col > 0)
    def _():
        gather_copy(col, below, gather_send.at[col]).wait_send()

    @pl.when(col < n_col - 1)
    def _():
        gather_copy(col, above, own_send).wait_send()

    def drain(k, carry):
        block = block_at(k)

        @pl.when(
            jnp.logical_or(
                jnp.logical_and(block > col, col > 0),
                jnp.logical_and(block < col, col < n_col - 1),
            )
        )
        def _():
            gather_copy(block, below, gather_send.at[block]).wait_send()

        @pl.when(block != col)
        def _():
            turn_copy(block).wait_send()

        for d in range(1, n_row):
            sum_copy(block, d).wait_send()
            full_copy(block, d).wait_send()
        return carry

    lax.fori_loop(0, n_col, drain, 0)
    for d in range(1, n_row):
        square_copy(d).wait_send()
        stat_copy(d).wait_send()
        out_copy(peer(d)).wait_send()
    hand.wait()


def shards(n_sec, n_row, n_col, hidden_in, norm_gain, q_weight, kv_weight, kv_cache, lengths):
    _, rows, width = hidden_in.shape
    _, prompts, positions, _, cache_width = kv_cache.shape
    kv_heads = cache_width // HEAD_DIM
    heads_per = q_weight.shape[2] // HEAD_DIM
    pairs_per = kv_weight.shape[2] // HEAD_DIM
    units = -(-(heads_per + pairs_per) // 4) * 4
    quarter = units // n_row
    group = heads_per * n_col // kv_heads
    tall = group * (rows // prompts)
    mine = kv_heads // n_row
    tiles = units * HEAD_DIM // TILE
    dims = (n_sec, n_row, n_col, units, quarter, heads_per, pairs_per, kv_heads)
    dma = pltpu.SemaphoreType.DMA
    vmem = pl.BlockSpec(memory_space=pltpu.VMEM)
    anywhere = pl.BlockSpec(memory_space=pl.ANY)
    handed, new_kv = pl.pallas_call(
        functools.partial(kernel, dims),
        out_shape=(
            jax.ShapeDtypeStruct((rows, heads_per * n_col // n_row * HEAD_DIM), BF16),
            jax.ShapeDtypeStruct((rows, 2 * cache_width), BF16),
        ),
        in_specs=[
            vmem,
            vmem,
            anywhere,
            anywhere,
            anywhere,
            pl.BlockSpec(memory_space=pltpu.SMEM),
        ],
        out_specs=(vmem, vmem),
        scratch_shapes=[
            pltpu.VMEM((tiles, width, TILE), BF16),
            pltpu.VMEM((prompts, 2 * positions, cache_width), BF16),
            pltpu.VMEM((n_col, rows, width), BF16),
            pltpu.VMEM((n_col, units, rows, HEAD_DIM), BF16),
            pltpu.VMEM((n_col, n_row, quarter, rows, HEAD_DIM), BF16),
            pltpu.VMEM((n_col, quarter, rows, HEAD_DIM), BF16),
            pltpu.VMEM((n_col * units, rows, HEAD_DIM), BF16),
            pltpu.VMEM((kv_heads, prompts, tall, HEAD_DIM), BF16),
            pltpu.VMEM((n_row, mine, prompts, tall, HEAD_DIM), BF16),
            pltpu.VMEM((tall, HEAD_DIM), F32),
            pltpu.VMEM((HEAD_DIM, tall), F32),
            pltpu.VMEM((HEAD_DIM, tall), F32),
            pltpu.VMEM((n_row, rows, HEAD_DIM), F32),
            pltpu.VMEM((rows, heads_per * n_col // n_row * HEAD_DIM), BF16),
            dma((tiles,)),
            dma,
            dma((n_col,)),
            dma((n_col,)),
            dma,
            dma((n_col, n_row)),
            dma((n_col, n_row)),
            dma((n_col,)),
            dma((n_col,)),
            dma((n_col, n_row)),
            dma((n_col, n_row)),
            dma((n_row,)),
            dma((n_row,)),
            dma((n_row,)),
            dma((n_row,)),
            dma((n_row,)),
            dma((n_row,)),
            dma,
            dma,
        ],
        compiler_params=pltpu.CompilerParams(
            collective_id=0, has_side_effects=True, vmem_limit_bytes=48 * 1024 * 1024
        ),
    )(
        hidden_in[0],
        norm_gain,
        q_weight[0],
        kv_weight[0],
        kv_cache[0].reshape(prompts, 2 * positions, cache_width),
        lengths,
    )
    return handed[None], new_kv[None]


def solution(mesh):
    n_sec, n_row, n_col = (mesh.shape[name] for name in ("section", "row", "col"))
    return jax.shard_map(
        functools.partial(shards, n_sec, n_row, n_col),
        mesh=mesh,
        in_specs=(
            P("section", "col", "row"),
            P("section", "row"),
            P("section", "row", "col"),
            P("section", "row", "col"),
            P("section", "col", "row", None, None),
            P("section", "col"),
        ),
        out_specs=(P("section", "col", "row"), P("section", "col", None)),
        check_vma=False,
    )
```

```python
import functools

import jax
import jax.numpy as jnp
from jax import lax
from jax.experimental import pallas as pl
from jax.experimental.pallas import tpu as pltpu
from jax.sharding import PartitionSpec as P

HEAD_DIM = 128
EPSILON = 1e-05
FLOOR = -1e30
TILE = 512
MESH = pl.DeviceIdType.MESH
F32 = jnp.float32
BF16 = jnp.bfloat16


def kernel(
    dims,
    hidden_ref,
    gain_ref,
    qw_ref,
    kvw_ref,
    cache_ref,
    len_ref,
    handed_ref,
    newkv_ref,
    weights,
    cache,
    keys,
    values,
    gathered,
    parts,
    arrived,
    summed,
    full,
    outs,
    outs_in,
    stat_rows,
    stat_in,
    squares,
    final,
    weight_sem,
    cache_sem,
    gather_send,
    gather_recv,
    own_send,
    sum_send,
    sum_recv,
    turn_send,
    turn_recv,
    full_send,
    full_recv,
    out_send,
    out_recv,
    stat_send,
    stat_recv,
    square_send,
    square_recv,
    hand_send,
    hand_recv,
):
    n_sec, n_row, n_col, units, quarter, heads_per, pairs_per, kv_heads = dims
    sec, row, col = lax.axis_index("section"), lax.axis_index("row"), lax.axis_index("col")
    rows, width = hidden_ref.shape
    prompts, positions = cache_ref.shape[0], cache_ref.shape[1]
    samples = rows // prompts
    group = (heads_per * n_col) // kv_heads
    tall = group * samples
    mine = kv_heads // n_row
    q_tiles = qw_ref.shape[1] // TILE
    tiles = units * HEAD_DIM // TILE
    pair_cols = kvw_ref.shape[1]

    mate = row + 1 - 2 * (row % 2)
    across = (row + 2) % 4
    far_peer = (mate + 2) % 4

    def peer(d):
        return lax.rem(row + d, n_row)

    loads = []
    for t in range(q_tiles):
        loads.append(
            pltpu.make_async_copy(
                qw_ref.at[:, pl.ds(t * TILE, TILE)], weights.at[t], weight_sem.at[t]
            )
        )
    for t in range(q_tiles, tiles):
        first = (t - q_tiles) * TILE
        wide = min(TILE, pair_cols - first)
        if wide > 0:
            loads.append(
                pltpu.make_async_copy(
                    kvw_ref.at[:, pl.ds(first, wide)],
                    weights.at[t, :, pl.ds(0, wide)],
                    weight_sem.at[t],
                )
            )
        else:
            loads.append(None)
    cache_load = pltpu.make_async_copy(cache_ref, cache, cache_sem)
    cache_load.start()
    for load in loads:
        if load is not None:
            load.start()

    barrier = pltpu.get_barrier_semaphore()
    for d in range(1, n_row):
        pl.semaphore_signal(barrier, inc=1, device_id=(sec, peer(d), col), device_id_type=MESH)
    for d in range(1, n_col):
        pl.semaphore_signal(
            barrier, inc=1, device_id=(sec, row, lax.rem(col + d, n_col)), device_id_type=MESH
        )
    pl.semaphore_signal(
        barrier, inc=1, device_id=(lax.rem(sec + n_sec - 1, n_sec), row, col), device_id_type=MESH
    )

    for t in range(q_tiles, tiles):
        first = (t - q_tiles) * TILE
        wide = max(0, min(TILE, pair_cols - first))
        if wide < TILE:
            weights[t, :, wide:] = jnp.zeros((width, TILE - wide), BF16)
    widened = hidden_ref[...].astype(F32)
    gathered[col] = (widened * gain_ref[...]).astype(BF16)
    squares[row] = jnp.broadcast_to(
        jnp.sum(widened * widened, axis=1, keepdims=True), (rows, HEAD_DIM)
    )

    pl.semaphore_wait(barrier, n_row - 1 + n_col - 1 + 1)

    def gather_copy(block, to, send_sem):
        return pltpu.make_async_remote_copy(
            src_ref=gathered.at[block],
            dst_ref=gathered.at[block],
            send_sem=send_sem,
            recv_sem=gather_recv.at[block],
            device_id=(sec, row, to),
            device_id_type=MESH,
        )

    below, above = jnp.maximum(col - 1, 0), jnp.minimum(col + 1, n_col - 1)

    @pl.when(col > 0)
    def _():
        gather_copy(col, below, gather_send.at[col]).start()

    @pl.when(col < n_col - 1)
    def _():
        gather_copy(col, above, own_send).start()

    def square_copy(d):
        return pltpu.make_async_remote_copy(
            src_ref=squares.at[row],
            dst_ref=squares.at[row],
            send_sem=square_send.at[d],
            recv_sem=square_recv.at[row],
            device_id=(sec, peer(d), col),
            device_id_type=MESH,
        )

    for d in range(1, n_row):
        square_copy(d).start()

    slots = 2 * positions
    picked = lax.broadcasted_iota(jnp.int32, (slots, slots), 0)
    offered = lax.broadcasted_iota(jnp.int32, (slots, slots), 1)
    wanted = jnp.where(picked < positions, 2 * picked, 2 * (picked - positions) + 1)
    pick = jnp.where(offered == wanted, 1.0, 0.0).astype(BF16)
    cache_load.wait()
    strip = 2 * HEAD_DIM
    strips = cache_ref.shape[3] // strip

    def split(k, carry):
        p = k // strips
        some = pl.ds(pl.multiple_of((k % strips) * strip, strip), strip)
        both = cache[p, :, :, some].reshape(slots, strip)
        apart = jnp.dot(pick, both, preferred_element_type=F32).astype(BF16)
        keys[p, :, some] = apart[:positions]
        values[p, :, some] = apart[positions:]
        return carry

    lax.fori_loop(0, prompts * strips, split, 0)

    shorter = jnp.minimum(col, n_col - 1 - col)
    upward = col < n_col - 1 - col

    def block_at(k):
        half = (k + 1) // 2
        near = jnp.where(k % 2 == 1, col + half, col - half)
        far = jnp.where(upward, col + (k - shorter), col - (k - shorter))
        return jnp.where(k <= 2 * shorter, near, far)

    def sum_copy(block, d):
        other = peer(d)
        return pltpu.make_async_remote_copy(
            src_ref=parts.at[block, pl.ds(other * quarter, quarter)],
            dst_ref=arrived.at[block, row],
            send_sem=sum_send.at[block, d],
            recv_sem=sum_recv.at[block, row],
            device_id=(sec, other, col),
            device_id_type=MESH,
        )

    def sum_wait(block, d):
        other = peer(d)
        pltpu.make_async_remote_copy(
            src_ref=arrived.at[block, other],
            dst_ref=arrived.at[block, other],
            send_sem=sum_send.at[block, d],
            recv_sem=sum_recv.at[block, other],
            device_id=(sec, other, col),
            device_id_type=MESH,
        ).wait_recv()

    def full_part(source, part):
        return full.at[pl.ds(source * units + part * quarter, quarter)]

    def full_copy(source, part, to, sem):
        return pltpu.make_async_remote_copy(
            src_ref=full_part(source, part),
            dst_ref=full_part(source, part),
            send_sem=full_send.at[source, sem],
            recv_sem=full_recv.at[source, part],
            device_id=(sec, to, col),
            device_id_type=MESH,
        )

    def spread(source):
        full_copy(source, row, across, 0).start()
        full_copy(source, row, mate, 1).start()

    def relay(source):
        full_copy(source, across, mate, 2).wait_recv()
        full_copy(source, across, mate, 2).start()

    def turn_copy(block):
        return pltpu.make_async_remote_copy(
            src_ref=summed.at[block],
            dst_ref=full_part(col, row),
            send_sem=turn_send.at[block],
            recv_sem=turn_recv.at[col],
            device_id=(sec, row, block),
            device_id_type=MESH,
        )

    def reduce_block(block):
        total = parts[block, pl.ds(row * quarter, quarter)].astype(F32)
        for d in range(1, n_row):
            sum_wait(block, d)
            total = total + arrived[block, peer(d)].astype(F32)
        total = total.astype(BF16)

        @pl.when(block == col)
        def _():
            full[pl.ds(col * units + row * quarter, quarter)] = total
            spread(col)

        @pl.when(block != col)
        def _():
            summed[block] = total
            turn_copy(block).start()

    def step(k, carry):
        block = block_at(k)

        @pl.when(k > 0)
        def _():
            gather_copy(block, below, gather_send.at[block]).wait_recv()

        @pl.when(jnp.logical_and(block > col, col > 0))
        def _():
            gather_copy(block, below, gather_send.at[block]).start()

        @pl.when(jnp.logical_and(block < col, col < n_col - 1))
        def _():
            gather_copy(block, above, gather_send.at[block]).start()

        for t in range(tiles):
            if loads[t] is not None:

                @pl.when(k == 0)
                def _():
                    loads[t].wait()

            product = jnp.dot(gathered[block], weights[t], preferred_element_type=F32)
            product = product.astype(BF16)
            for u in range(TILE // HEAD_DIM):
                parts[block, t * (TILE // HEAD_DIM) + u] = product[
                    :, u * HEAD_DIM : (u + 1) * HEAD_DIM
                ]
        for d in range(1, n_row):
            sum_copy(block, d).start()

        @pl.when(k > 0)
        def _():
            reduce_block(block_at(k - 1))

        return carry

    lax.fori_loop(0, n_col, step, 0)
    reduce_block(block_at(n_col - 1))

    def forward(k, carry):
        source = block_at(k)
        pltpu.make_async_remote_copy(
            src_ref=full_part(source, row),
            dst_ref=full_part(source, row),
            send_sem=turn_send.at[source],
            recv_sem=turn_recv.at[source],
            device_id=(sec, row, source),
            device_id_type=MESH,
        ).wait_recv()
        spread(source)
        relay(block_at(k - 1))
        return carry

    lax.fori_loop(1, n_col, forward, 0)
    relay(block_at(n_col - 1))

    for d in range(1, n_row):
        other = peer(d)
        pltpu.make_async_remote_copy(
            src_ref=squares.at[other],
            dst_ref=squares.at[other],
            send_sem=square_send.at[d],
            recv_sem=square_recv.at[other],
            device_id=(sec, other, col),
            device_id_type=MESH,
        ).wait_recv()
    square_sum = squares[0]
    for i in range(1, n_row):
        square_sum = square_sum + squares[i]
    scaling = lax.rsqrt(square_sum / (width * n_row) + EPSILON)

    def head_unit(head):
        return (head // heads_per) * units + head % heads_per

    def pair_unit(pair):
        return (pair // pairs_per) * units + heads_per + pair % pairs_per

    def scaled(unit, p):
        some = pl.ds(p * samples, samples)
        factor = scaling[p * samples : (p + 1) * samples]
        return (full[unit, some, :].astype(F32) * factor).astype(BF16)

    def queries(g, p):
        return jnp.concatenate([scaled(head_unit(g * group + i), p) for i in range(group)], axis=0)

    score_scale = HEAD_DIM ** (-0.5)
    lane = lax.broadcasted_iota(jnp.int32, (tall, HEAD_DIM), 1)
    position = row * positions + lax.broadcasted_iota(jnp.int32, (1, positions), 1)
    valid = [position < len_ref[0, p] for p in range(prompts)]

    def attend(heads):
        pairs = [(g, p) for g in heads for p in range(prompts)]

        def some(g):
            return pl.ds(pl.multiple_of(g * HEAD_DIM, HEAD_DIM), HEAD_DIM)

        scores = [
            lax.dot_general(
                queries(g, p),
                keys[p, :, some(g)],
                (((1,), (1,)), ((), ())),
                preferred_element_type=F32,
            )
            for g, p in pairs
        ]
        scores = [
            jnp.where(valid[p], score * score_scale, FLOOR)
            for (g, p), score in zip(pairs, scores)
        ]
        tops = [jnp.max(score, axis=1, keepdims=True) for score in scores]
        raised = [
            jnp.where(valid[p], jnp.exp(score - top), 0.0)
            for (g, p), score, top in zip(pairs, scores, tops)
        ]
        totals = [jnp.sum(weight, axis=1, keepdims=True) for weight in raised]
        products = [
            jnp.dot(weight.astype(BF16), values[p, :, some(g)], preferred_element_type=F32)
            for (g, p), weight in zip(pairs, raised)
        ]
        for (g, p), product in zip(pairs, products):
            outs[g, p] = product.astype(BF16)
        for i, g in enumerate(heads):
            tile = jnp.zeros((tall, HEAD_DIM), F32)
            for p in range(prompts):
                tile = jnp.where(lane == 2 * p, tops[i * prompts + p], tile)
                tile = jnp.where(lane == 2 * p + 1, totals[i * prompts + p], tile)
            stat_rows[g] = tile.T[:8]

    def out_copy(dest):
        return pltpu.make_async_remote_copy(
            src_ref=outs.at[pl.ds(dest * mine, mine)],
            dst_ref=outs_in.at[row],
            send_sem=out_send.at[dest],
            recv_sem=out_recv.at[row],
            device_id=(sec, dest, col),
            device_id_type=MESH,
        )

    chunk_heads = max(1, heads_per // group)
    chunk_cols = max(1, group // heads_per)
    chunks = kv_heads // chunk_heads
    by_dest = chunks == n_row and chunk_heads == mine

    def stat_copy(dest):
        return pltpu.make_async_remote_copy(
            src_ref=stat_rows.at[pl.ds(dest * mine, mine)],
            dst_ref=stat_in.at[row],
            send_sem=stat_send.at[dest],
            recv_sem=stat_recv.at[row],
            device_id=(sec, dest, col),
            device_id_type=MESH,
        )

    def chunk(k, carry):
        j = k
        if by_dest:
            j = jnp.where(k == 0, across, jnp.where(k == 1, far_peer, jnp.where(k == 2, mate, row)))
        for i in range(chunk_cols):
            source = j * chunk_cols + i
            full_copy(source, mate, mate, 1).wait_recv()
            full_copy(source, far_peer, mate, 2).wait_recv()
        attend([j * chunk_heads + i for i in range(chunk_heads)])
        last = j * chunk_heads + chunk_heads - 1
        dest = last // mine

        @pl.when(jnp.logical_and(last % mine == mine - 1, dest != row))
        def _():
            out_copy(dest).start()
            stat_copy(dest).start()

        return carry

    lax.fori_loop(0, chunks, chunk, 0)

    outs_in[row] = outs[pl.ds(row * mine, mine)]
    stat_in[row] = stat_rows[pl.ds(row * mine, mine)]

    for pair in range(2 * kv_heads):
        newkv_ref[:, pair * HEAD_DIM : (pair + 1) * HEAD_DIM] = (
            full[pair_unit(pair)].astype(F32) * scaling
        ).astype(BF16)

    def own_part(g, p):
        new_key = jnp.concatenate([scaled(pair_unit(g), p)] * group, axis=0)
        product = queries(g, p).astype(F32) * new_key.astype(F32)
        return jnp.sum(product, axis=1, keepdims=True) * score_scale

    own_scores = [[own_part(row * mine + i, p) for p in range(prompts)] for i in range(mine)]

    for d in range(1, n_row):
        other = peer(d)
        pltpu.make_async_remote_copy(
            src_ref=stat_in.at[other],
            dst_ref=stat_in.at[other],
            send_sem=stat_send.at[other],
            recv_sem=stat_recv.at[other],
            device_id=(sec, other, col),
            device_id_type=MESH,
        ).wait_recv()
        pltpu.make_async_remote_copy(
            src_ref=outs_in.at[other],
            dst_ref=outs_in.at[other],
            send_sem=out_send.at[other],
            recv_sem=out_recv.at[other],
            device_id=(sec, other, col),
            device_id_type=MESH,
        ).wait_recv()

    lines = stat_in[...].reshape(n_row * mine * 8, tall)
    stats = jnp.concatenate([lines, jnp.zeros((HEAD_DIM - n_row * mine * 8, tall), F32)], axis=0).T
    span = group * HEAD_DIM

    def hand_copy(i):
        return pltpu.make_async_remote_copy(
            src_ref=final.at[:, pl.ds(i * span, span)],
            dst_ref=handed_ref.at[:, pl.ds(i * span, span)],
            send_sem=hand_send.at[i],
            recv_sem=hand_recv.at[i],
            device_id=(lax.rem(sec + 1, n_sec), row, col),
            device_id_type=MESH,
        )

    for i in range(mine):
        g = row * mine + i
        for p in range(prompts):
            new_value = jnp.concatenate([scaled(pair_unit(kv_heads + g), p)] * group, axis=0)
            own = own_scores[i][p]
            top = own
            tops, totals = [], []
            for s in range(n_row):
                at = (s * mine + i) * 8 + 2 * p
                tops.append(stats[:, at : at + 1])
                totals.append(stats[:, at + 1 : at + 2])
                top = jnp.maximum(top, tops[-1])
            own_weight = jnp.exp(own - top)
            total = own_weight
            value = own_weight.astype(BF16).astype(F32) * new_value.astype(F32)
            for s in range(n_row):
                keep = jnp.exp(tops[s] - top)
                total = total + keep * totals[s]
                value = value + keep * outs_in[s, i, p].astype(F32)
            done = (value / total).astype(BF16)
            for h in range(group):
                first = (i * group + h) * HEAD_DIM
                final[p * samples : (p + 1) * samples, first : first + HEAD_DIM] = done[
                    h * samples : (h + 1) * samples
                ]
        hand_copy(i).start()

    @pl.when(col > 0)
    def _():
        gather_copy(col, below, gather_send.at[col]).wait_send()

    @pl.when(col < n_col - 1)
    def _():
        gather_copy(col, above, own_send).wait_send()

    def drain(k, carry):
        block = block_at(k)

        @pl.when(
            jnp.logical_or(
                jnp.logical_and(block > col, col > 0),
                jnp.logical_and(block < col, col < n_col - 1),
            )
        )
        def _():
            gather_copy(block, below, gather_send.at[block]).wait_send()

        @pl.when(block != col)
        def _():
            turn_copy(block).wait_send()

        for d in range(1, n_row):
            sum_copy(block, d).wait_send()
        full_copy(block, row, across, 0).wait_send()
        full_copy(block, row, mate, 1).wait_send()
        full_copy(block, across, mate, 2).wait_send()
        return carry

    lax.fori_loop(0, n_col, drain, 0)
    for d in range(1, n_row):
        square_copy(d).wait_send()
        stat_copy(peer(d)).wait_send()
        out_copy(peer(d)).wait_send()
    for i in range(mine):
        hand_copy(i).wait()


def shards(n_sec, n_row, n_col, hidden_in, norm_gain, q_weight, kv_weight, kv_cache, lengths):
    _, rows, width = hidden_in.shape
    _, prompts, positions, _, cache_width = kv_cache.shape
    kv_heads = cache_width // HEAD_DIM
    heads_per = q_weight.shape[2] // HEAD_DIM
    pairs_per = kv_weight.shape[2] // HEAD_DIM
    units = -(-(heads_per + pairs_per) // 4) * 4
    quarter = units // n_row
    group = heads_per * n_col // kv_heads
    tall = group * (rows // prompts)
    mine = kv_heads // n_row
    tiles = units * HEAD_DIM // TILE
    dims = (n_sec, n_row, n_col, units, quarter, heads_per, pairs_per, kv_heads)
    dma = pltpu.SemaphoreType.DMA
    vmem = pl.BlockSpec(memory_space=pltpu.VMEM)
    anywhere = pl.BlockSpec(memory_space=pl.ANY)
    handed, new_kv = pl.pallas_call(
        functools.partial(kernel, dims),
        out_shape=(
            jax.ShapeDtypeStruct((rows, heads_per * n_col // n_row * HEAD_DIM), BF16),
            jax.ShapeDtypeStruct((rows, 2 * cache_width), BF16),
        ),
        in_specs=[
            vmem,
            vmem,
            anywhere,
            anywhere,
            anywhere,
            pl.BlockSpec(memory_space=pltpu.SMEM),
        ],
        out_specs=(vmem, vmem),
        scratch_shapes=[
            pltpu.VMEM((tiles, width, TILE), BF16),
            pltpu.VMEM((prompts, positions, 2, cache_width), BF16),
            pltpu.VMEM((prompts, positions, cache_width), BF16),
            pltpu.VMEM((prompts, positions, cache_width), BF16),
            pltpu.VMEM((n_col, rows, width), BF16),
            pltpu.VMEM((n_col, units, rows, HEAD_DIM), BF16),
            pltpu.VMEM((n_col, n_row, quarter, rows, HEAD_DIM), BF16),
            pltpu.VMEM((n_col, quarter, rows, HEAD_DIM), BF16),
            pltpu.VMEM((n_col * units, rows, HEAD_DIM), BF16),
            pltpu.VMEM((kv_heads, prompts, tall, HEAD_DIM), BF16),
            pltpu.VMEM((n_row, mine, prompts, tall, HEAD_DIM), BF16),
            pltpu.VMEM((kv_heads, 8, tall), F32),
            pltpu.VMEM((n_row, mine, 8, tall), F32),
            pltpu.VMEM((n_row, rows, HEAD_DIM), F32),
            pltpu.VMEM((rows, heads_per * n_col // n_row * HEAD_DIM), BF16),
            dma((tiles,)),
            dma,
            dma((n_col,)),
            dma((n_col,)),
            dma,
            dma((n_col, n_row)),
            dma((n_col, n_row)),
            dma((n_col,)),
            dma((n_col,)),
            dma((n_col, n_row)),
            dma((n_col, n_row)),
            dma((n_row,)),
            dma((n_row,)),
            dma((n_row,)),
            dma((n_row,)),
            dma((n_row,)),
            dma((n_row,)),
            dma((mine,)),
            dma((mine,)),
        ],
        compiler_params=pltpu.CompilerParams(
            collective_id=0, has_side_effects=True, vmem_limit_bytes=60 * 1024 * 1024
        ),
    )(
        hidden_in[0],
        norm_gain,
        q_weight[0],
        kv_weight[0],
        kv_cache[0],
        lengths,
    )
    return handed[None], new_kv[None]


def solution(mesh):
    n_sec, n_row, n_col = (mesh.shape[name] for name in ("section", "row", "col"))
    return jax.shard_map(
        functools.partial(shards, n_sec, n_row, n_col),
        mesh=mesh,
        in_specs=(
            P("section", "col", "row"),
            P("section", "row"),
            P("section", "row", "col"),
            P("section", "row", "col"),
            P("section", "col", "row", None, None),
            P("section", "col"),
        ),
        out_specs=(P("section", "col", "row"), P("section", "col", None)),
        check_vma=False,
    )
```

```python
import functools

import jax
import jax.numpy as jnp
from jax import lax
from jax.experimental import pallas as pl
from jax.experimental.pallas import tpu as pltpu
from jax.sharding import PartitionSpec as P

HEAD_DIM = 128
EPSILON = 1e-05
FLOOR = -1e30
MESH = pl.DeviceIdType.MESH
F32 = jnp.float32
BF16 = jnp.bfloat16


def kernel(
    dims,
    hidden_ref,
    gain_ref,
    qw_ref,
    kvw_ref,
    cache_ref,
    len_ref,
    handed_ref,
    newkv_ref,
    weights,
    cache,
    keys,
    values,
    gathered,
    parts,
    arrived,
    summed,
    full,
    outs,
    outs_in,
    stat_rows,
    stat_in,
    squares,
    final,
    weight_sem,
    cache_sem,
    gather_send,
    gather_recv,
    own_send,
    sum_send,
    sum_recv,
    turn_send,
    turn_recv,
    full_send,
    full_recv,
    out_send,
    out_recv,
    stat_send,
    stat_recv,
    square_send,
    square_recv,
    hand_send,
    hand_recv,
):
    n_sec, n_row, n_col, units, quarter, heads_per, pairs_per, kv_heads = dims
    sec, row, col = lax.axis_index("section"), lax.axis_index("row"), lax.axis_index("col")
    rows, width = hidden_ref.shape
    prompts, positions = cache_ref.shape[0], cache_ref.shape[1]
    samples = rows // prompts
    group = (heads_per * n_col) // kv_heads
    tall = group * samples
    mine = kv_heads // n_row
    tile = quarter * HEAD_DIM
    half = width // 2
    is_end = jnp.logical_or(col == 0, col == n_col - 1)

    mate = row + 1 - 2 * (row % 2)
    across = (row + 2) % 4
    far_peer = (mate + 2) % 4

    def peer(d):
        return lax.rem(row + d, n_row)

    cache_load = pltpu.make_async_copy(cache_ref, cache, cache_sem)
    cache_load.start()
    loads, filled = [], 0
    for source in (qw_ref, kvw_ref):
        taken = 0
        while taken < source.shape[1]:
            t, at = filled // tile, filled % tile
            wide = min(source.shape[1] - taken, tile - at)
            loads.append(
                pltpu.make_async_copy(
                    source.at[:, pl.ds(taken, wide)],
                    weights.at[t, :, pl.ds(at, wide)],
                    weight_sem.at[len(loads)],
                )
            )
            taken, filled = taken + wide, filled + wide
    for load in loads:
        load.start()

    barrier = pltpu.get_barrier_semaphore()
    for d in range(1, n_row):
        pl.semaphore_signal(barrier, inc=1, device_id=(sec, peer(d), col), device_id_type=MESH)
    for d in range(1, n_col):
        pl.semaphore_signal(
            barrier, inc=1, device_id=(sec, row, lax.rem(col + d, n_col)), device_id_type=MESH
        )
    pl.semaphore_signal(
        barrier, inc=1, device_id=(lax.rem(sec + n_sec - 1, n_sec), row, col), device_id_type=MESH
    )

    while filled < n_row * tile:
        t, at = filled // tile, filled % tile
        weights[t, :, at:] = jnp.zeros((width, tile - at), BF16)
        filled = (t + 1) * tile
    widened = hidden_ref[...].astype(F32)
    for h in range(2):
        some = slice(h * half, (h + 1) * half)
        gathered[col, h] = (widened[:, some] * gain_ref[:, some]).astype(BF16)
    squares[row] = jnp.broadcast_to(
        jnp.sum(widened * widened, axis=1, keepdims=True), (rows, HEAD_DIM)
    )

    pl.semaphore_wait(barrier, n_row - 1 + n_col - 1 + 1)

    def gather_copy(block, h, to, send_sem):
        return pltpu.make_async_remote_copy(
            src_ref=gathered.at[block, h],
            dst_ref=gathered.at[block, h],
            send_sem=send_sem.at[h],
            recv_sem=gather_recv.at[block, h],
            device_id=(sec, row, to),
            device_id_type=MESH,
        )

    below, above = jnp.maximum(col - 1, 0), jnp.minimum(col + 1, n_col - 1)

    for h in range(2):

        @pl.when(col > 0)
        def _():
            gather_copy(col, h, below, gather_send.at[col]).start()

        @pl.when(col < n_col - 1)
        def _():
            gather_copy(col, h, above, own_send).start()

    def square_copy(d):
        return pltpu.make_async_remote_copy(
            src_ref=squares.at[row],
            dst_ref=squares.at[row],
            send_sem=square_send.at[d],
            recv_sem=square_recv.at[row],
            device_id=(sec, peer(d), col),
            device_id_type=MESH,
        )

    for d in range(1, n_row):
        square_copy(d).start()

    slots = 2 * positions
    picked = lax.broadcasted_iota(jnp.int32, (slots, slots), 0)
    offered = lax.broadcasted_iota(jnp.int32, (slots, slots), 1)
    wanted = jnp.where(picked < positions, 2 * picked, 2 * (picked - positions) + 1)
    pick = jnp.where(offered == wanted, 1.0, 0.0).astype(BF16)
    cache_load.wait()
    strip = 2 * HEAD_DIM
    strips = cache_ref.shape[3] // strip

    def split(k, carry):
        p = k // strips
        some = pl.ds(pl.multiple_of((k % strips) * strip, strip), strip)
        both = cache[p, :, :, some].reshape(slots, strip)
        apart = jnp.dot(pick, both, preferred_element_type=F32).astype(BF16)
        keys[p, :, some] = apart[:positions]
        values[p, :, some] = apart[positions:]
        return carry

    lax.fori_loop(0, prompts * strips, split, 0)

    shorter = jnp.minimum(col, n_col - 1 - col)
    upward = col < n_col - 1 - col

    def block_at(k):
        away = (k + 1) // 2
        near = jnp.where(k % 2 == 1, col + away, col - away)
        far = jnp.where(upward, col + (k - shorter), col - (k - shorter))
        return jnp.where(k <= 2 * shorter, near, far)

    def pass_on(k, h):
        block = block_at(k)
        gather_copy(block, h, below, gather_send.at[block]).wait_recv()

        @pl.when(block > col)
        def _():
            gather_copy(block, h, below, gather_send.at[block]).start()

        @pl.when(block < col)
        def _():
            gather_copy(block, h, above, gather_send.at[block]).start()

    @pl.when(jnp.logical_not(is_end))
    def _():
        for first in range(1, n_col, 2):
            for h in range(2):
                for k in range(first, min(first + 2, n_col)):
                    pass_on(k, h)

    def sum_copy(block, other):
        return pltpu.make_async_remote_copy(
            src_ref=parts.at[block, pl.ds(other * quarter, quarter)],
            dst_ref=arrived.at[block, row],
            send_sem=sum_send.at[block, other],
            recv_sem=sum_recv.at[block, row],
            device_id=(sec, other, col),
            device_id_type=MESH,
        )

    def sum_wait(block, d):
        other = peer(d)
        pltpu.make_async_remote_copy(
            src_ref=arrived.at[block, other],
            dst_ref=arrived.at[block, other],
            send_sem=sum_send.at[block, d],
            recv_sem=sum_recv.at[block, other],
            device_id=(sec, other, col),
            device_id_type=MESH,
        ).wait_recv()

    def full_part(source, part):
        return full.at[pl.ds(source * units + part * quarter, quarter)]

    def full_copy(source, part, to, sem):
        return pltpu.make_async_remote_copy(
            src_ref=full_part(source, part),
            dst_ref=full_part(source, part),
            send_sem=full_send.at[source, sem],
            recv_sem=full_recv.at[source, part],
            device_id=(sec, to, col),
            device_id_type=MESH,
        )

    def spread(source):
        full_copy(source, row, across, 0).start()
        full_copy(source, row, mate, 1).start()

    def relay(source):
        full_copy(source, across, mate, 2).wait_recv()
        full_copy(source, across, mate, 2).start()

    def turn_copy(block):
        return pltpu.make_async_remote_copy(
            src_ref=summed.at[block],
            dst_ref=full_part(col, row),
            send_sem=turn_send.at[block],
            recv_sem=turn_recv.at[col],
            device_id=(sec, row, block),
            device_id_type=MESH,
        )

    def reduce_block(block):
        total = parts[block, pl.ds(row * quarter, quarter)].astype(F32)
        for d in range(1, n_row):
            sum_wait(block, d)
            total = total + arrived[block, peer(d)].astype(F32)
        total = total.astype(BF16)

        @pl.when(block == col)
        def _():
            full[pl.ds(col * units + row * quarter, quarter)] = total
            spread(col)

        @pl.when(block != col)
        def _():
            summed[block] = total
            turn_copy(block).start()

    for load in loads:
        load.wait()

    step_blocks = 2

    def target(j):
        return jnp.where(
            j == 0, across, jnp.where(j == 1, far_peer, jnp.where(j == 2, mate, row))
        )

    def step(s, carry):
        blocks = [block_at(step_blocks * s + i) for i in range(step_blocks)]

        @pl.when(is_end)
        def _():
            for i, block in enumerate(blocks):

                @pl.when(step_blocks * s + i > 0)
                def _():
                    for h in range(2):
                        gather_copy(block, h, below, gather_send.at[block]).wait_recv()

        def multiply(j, carry):
            dest = target(j)
            product = jnp.zeros((step_blocks * rows, tile), F32)
            for h in range(2):
                taken = jnp.concatenate([gathered[block, h] for block in blocks], axis=0)
                product = product + jnp.dot(
                    taken, weights[dest, h * half : (h + 1) * half], preferred_element_type=F32
                )
            product = product.astype(BF16)
            for i, block in enumerate(blocks):
                for u in range(quarter):
                    parts[block, dest * quarter + u] = product[
                        i * rows : (i + 1) * rows, u * HEAD_DIM : (u + 1) * HEAD_DIM
                    ]

            @pl.when(j < n_row - 1)
            def _():
                for block in blocks:
                    sum_copy(block, dest).start()

            return carry

        lax.fori_loop(0, n_row // 2, multiply, 0)

        @pl.when(s > 0)
        def _():
            for i in range(step_blocks):
                reduce_block(block_at(step_blocks * (s - 1) + i))

        lax.fori_loop(n_row // 2, n_row, multiply, 0)
        return carry

    lax.fori_loop(0, n_col // step_blocks, step, 0)
    for i in range(step_blocks):
        reduce_block(block_at(n_col - step_blocks + i))

    def forward(k, carry):
        source = block_at(k)
        pltpu.make_async_remote_copy(
            src_ref=full_part(source, row),
            dst_ref=full_part(source, row),
            send_sem=turn_send.at[source],
            recv_sem=turn_recv.at[source],
            device_id=(sec, row, source),
            device_id_type=MESH,
        ).wait_recv()
        spread(source)
        relay(block_at(k - 1))
        return carry

    lax.fori_loop(1, n_col, forward, 0)
    relay(block_at(n_col - 1))

    for d in range(1, n_row):
        other = peer(d)
        pltpu.make_async_remote_copy(
            src_ref=squares.at[other],
            dst_ref=squares.at[other],
            send_sem=square_send.at[d],
            recv_sem=square_recv.at[other],
            device_id=(sec, other, col),
            device_id_type=MESH,
        ).wait_recv()
    square_sum = squares[0]
    for i in range(1, n_row):
        square_sum = square_sum + squares[i]
    scaling = lax.rsqrt(square_sum / (width * n_row) + EPSILON)

    def head_unit(head):
        return (head // heads_per) * units + head % heads_per

    def pair_unit(pair):
        return (pair // pairs_per) * units + heads_per + pair % pairs_per

    def scaled(unit, p):
        some = pl.ds(p * samples, samples)
        factor = scaling[p * samples : (p + 1) * samples]
        return (full[unit, some, :].astype(F32) * factor).astype(BF16)

    def queries(g, p):
        return jnp.concatenate([scaled(head_unit(g * group + i), p) for i in range(group)], axis=0)

    score_scale = HEAD_DIM ** (-0.5)
    lane = lax.broadcasted_iota(jnp.int32, (tall, HEAD_DIM), 1)
    position = row * positions + lax.broadcasted_iota(jnp.int32, (1, positions), 1)
    valid = [position < len_ref[0, p] for p in range(prompts)]

    def attend(heads):
        pairs = [(g, p) for g in heads for p in range(prompts)]

        def some(g):
            return pl.ds(pl.multiple_of(g * HEAD_DIM, HEAD_DIM), HEAD_DIM)

        scores = [
            lax.dot_general(
                queries(g, p),
                keys[p, :, some(g)],
                (((1,), (1,)), ((), ())),
                preferred_element_type=F32,
            )
            for g, p in pairs
        ]
        scores = [
            jnp.where(valid[p], score * score_scale, FLOOR)
            for (g, p), score in zip(pairs, scores)
        ]
        tops = [jnp.max(score, axis=1, keepdims=True) for score in scores]
        raised = [
            jnp.where(valid[p], jnp.exp(score - top), 0.0)
            for (g, p), score, top in zip(pairs, scores, tops)
        ]
        totals = [jnp.sum(weight, axis=1, keepdims=True) for weight in raised]
        products = [
            jnp.dot(weight.astype(BF16), values[p, :, some(g)], preferred_element_type=F32)
            for (g, p), weight in zip(pairs, raised)
        ]
        for (g, p), product in zip(pairs, products):
            outs[g, p] = product.astype(BF16)
        for i, g in enumerate(heads):
            both = jnp.zeros((tall, HEAD_DIM), F32)
            for p in range(prompts):
                both = jnp.where(lane == 2 * p, tops[i * prompts + p], both)
                both = jnp.where(lane == 2 * p + 1, totals[i * prompts + p], both)
            stat_rows[g] = both.T[:8]

    def out_copy(dest):
        return pltpu.make_async_remote_copy(
            src_ref=outs.at[pl.ds(dest * mine, mine)],
            dst_ref=outs_in.at[row],
            send_sem=out_send.at[dest],
            recv_sem=out_recv.at[row],
            device_id=(sec, dest, col),
            device_id_type=MESH,
        )

    chunk_heads = max(1, heads_per // group)
    chunk_cols = max(1, group // heads_per)
    chunks = kv_heads // chunk_heads
    by_dest = chunks == n_row and chunk_heads == mine

    def stat_copy(dest):
        return pltpu.make_async_remote_copy(
            src_ref=stat_rows.at[pl.ds(dest * mine, mine)],
            dst_ref=stat_in.at[row],
            send_sem=stat_send.at[dest],
            recv_sem=stat_recv.at[row],
            device_id=(sec, dest, col),
            device_id_type=MESH,
        )

    def chunk(k, carry):
        j = k
        if by_dest:
            j = target(k)
        for i in range(chunk_cols):
            source = j * chunk_cols + i
            full_copy(source, mate, mate, 1).wait_recv()
            full_copy(source, far_peer, mate, 2).wait_recv()
        attend([j * chunk_heads + i for i in range(chunk_heads)])
        last = j * chunk_heads + chunk_heads - 1
        dest = last // mine

        @pl.when(jnp.logical_and(last % mine == mine - 1, dest != row))
        def _():
            out_copy(dest).start()
            stat_copy(dest).start()

        return carry

    lax.fori_loop(0, chunks, chunk, 0)

    outs_in[row] = outs[pl.ds(row * mine, mine)]
    stat_in[row] = stat_rows[pl.ds(row * mine, mine)]

    for pair in range(2 * kv_heads):
        newkv_ref[:, pair * HEAD_DIM : (pair + 1) * HEAD_DIM] = (
            full[pair_unit(pair)].astype(F32) * scaling
        ).astype(BF16)

    def own_part(g, p):
        new_key = jnp.concatenate([scaled(pair_unit(g), p)] * group, axis=0)
        product = queries(g, p).astype(F32) * new_key.astype(F32)
        return jnp.sum(product, axis=1, keepdims=True) * score_scale

    own_scores = [[own_part(row * mine + i, p) for p in range(prompts)] for i in range(mine)]

    for d in range(1, n_row):
        other = peer(d)
        pltpu.make_async_remote_copy(
            src_ref=stat_in.at[other],
            dst_ref=stat_in.at[other],
            send_sem=stat_send.at[other],
            recv_sem=stat_recv.at[other],
            device_id=(sec, other, col),
            device_id_type=MESH,
        ).wait_recv()
        pltpu.make_async_remote_copy(
            src_ref=outs_in.at[other],
            dst_ref=outs_in.at[other],
            send_sem=out_send.at[other],
            recv_sem=out_recv.at[other],
            device_id=(sec, other, col),
            device_id_type=MESH,
        ).wait_recv()

    lines = stat_in[...].reshape(n_row * mine * 8, tall)
    stats = jnp.concatenate([lines, jnp.zeros((HEAD_DIM - n_row * mine * 8, tall), F32)], axis=0).T
    span = group * HEAD_DIM

    def hand_copy(i):
        return pltpu.make_async_remote_copy(
            src_ref=final.at[:, pl.ds(i * span, span)],
            dst_ref=handed_ref.at[:, pl.ds(i * span, span)],
            send_sem=hand_send.at[i],
            recv_sem=hand_recv.at[i],
            device_id=(lax.rem(sec + 1, n_sec), row, col),
            device_id_type=MESH,
        )

    for i in range(mine):
        g = row * mine + i
        for p in range(prompts):
            new_value = jnp.concatenate([scaled(pair_unit(kv_heads + g), p)] * group, axis=0)
            own = own_scores[i][p]
            top = own
            tops, totals = [], []
            for s in range(n_row):
                at = (s * mine + i) * 8 + 2 * p
                tops.append(stats[:, at : at + 1])
                totals.append(stats[:, at + 1 : at + 2])
                top = jnp.maximum(top, tops[-1])
            own_weight = jnp.exp(own - top)
            total = own_weight
            value = own_weight.astype(BF16).astype(F32) * new_value.astype(F32)
            for s in range(n_row):
                keep = jnp.exp(tops[s] - top)
                total = total + keep * totals[s]
                value = value + keep * outs_in[s, i, p].astype(F32)
            done = (value / total).astype(BF16)
            for h in range(group):
                first = (i * group + h) * HEAD_DIM
                final[p * samples : (p + 1) * samples, first : first + HEAD_DIM] = done[
                    h * samples : (h + 1) * samples
                ]
        hand_copy(i).start()

    for h in range(2):

        @pl.when(col > 0)
        def _():
            gather_copy(col, h, below, gather_send.at[col]).wait_send()

        @pl.when(col < n_col - 1)
        def _():
            gather_copy(col, h, above, own_send).wait_send()

    def drain(k, carry):
        block = block_at(k)

        @pl.when(jnp.logical_and(block != col, jnp.logical_not(is_end)))
        def _():
            for h in range(2):
                gather_copy(block, h, below, gather_send.at[block]).wait_send()

        @pl.when(block != col)
        def _():
            turn_copy(block).wait_send()

        for d in range(1, n_row):
            sum_copy(block, peer(d)).wait_send()
        full_copy(block, row, across, 0).wait_send()
        full_copy(block, row, mate, 1).wait_send()
        full_copy(block, across, mate, 2).wait_send()
        return carry

    lax.fori_loop(0, n_col, drain, 0)
    for d in range(1, n_row):
        square_copy(d).wait_send()
        stat_copy(peer(d)).wait_send()
        out_copy(peer(d)).wait_send()
    for i in range(mine):
        hand_copy(i).wait()


def shards(n_sec, n_row, n_col, hidden_in, norm_gain, q_weight, kv_weight, kv_cache, lengths):
    _, rows, width = hidden_in.shape
    _, prompts, positions, _, cache_width = kv_cache.shape
    kv_heads = cache_width // HEAD_DIM
    heads_per = q_weight.shape[2] // HEAD_DIM
    pairs_per = kv_weight.shape[2] // HEAD_DIM
    units = -(-(heads_per + pairs_per) // 4) * 4
    quarter = units // n_row
    group = heads_per * n_col // kv_heads
    tall = group * (rows // prompts)
    mine = kv_heads // n_row
    dims = (n_sec, n_row, n_col, units, quarter, heads_per, pairs_per, kv_heads)
    dma = pltpu.SemaphoreType.DMA
    vmem = pl.BlockSpec(memory_space=pltpu.VMEM)
    anywhere = pl.BlockSpec(memory_space=pl.ANY)
    handed, new_kv = pl.pallas_call(
        functools.partial(kernel, dims),
        out_shape=(
            jax.ShapeDtypeStruct((rows, heads_per * n_col // n_row * HEAD_DIM), BF16),
            jax.ShapeDtypeStruct((rows, 2 * cache_width), BF16),
        ),
        in_specs=[
            vmem,
            vmem,
            anywhere,
            anywhere,
            anywhere,
            pl.BlockSpec(memory_space=pltpu.SMEM),
        ],
        out_specs=(vmem, vmem),
        scratch_shapes=[
            pltpu.VMEM((n_row, width, quarter * HEAD_DIM), BF16),
            pltpu.VMEM((prompts, positions, 2, cache_width), BF16),
            pltpu.VMEM((prompts, positions, cache_width), BF16),
            pltpu.VMEM((prompts, positions, cache_width), BF16),
            pltpu.VMEM((n_col, 2, rows, width // 2), BF16),
            pltpu.VMEM((n_col, units, rows, HEAD_DIM), BF16),
            pltpu.VMEM((n_col, n_row, quarter, rows, HEAD_DIM), BF16),
            pltpu.VMEM((n_col, quarter, rows, HEAD_DIM), BF16),
            pltpu.VMEM((n_col * units, rows, HEAD_DIM), BF16),
            pltpu.VMEM((kv_heads, prompts, tall, HEAD_DIM), BF16),
            pltpu.VMEM((n_row, mine, prompts, tall, HEAD_DIM), BF16),
            pltpu.VMEM((kv_heads, 8, tall), F32),
            pltpu.VMEM((n_row, mine, 8, tall), F32),
            pltpu.VMEM((n_row, rows, HEAD_DIM), F32),
            pltpu.VMEM((rows, heads_per * n_col // n_row * HEAD_DIM), BF16),
            dma((2 * n_row + 2,)),
            dma,
            dma((n_col, 2)),
            dma((n_col, 2)),
            dma((2,)),
            dma((n_col, n_row)),
            dma((n_col, n_row)),
            dma((n_col,)),
            dma((n_col,)),
            dma((n_col, n_row)),
            dma((n_col, n_row)),
            dma((n_row,)),
            dma((n_row,)),
            dma((n_row,)),
            dma((n_row,)),
            dma((n_row,)),
            dma((n_row,)),
            dma((mine,)),
            dma((mine,)),
        ],
        compiler_params=pltpu.CompilerParams(
            collective_id=0, has_side_effects=True, vmem_limit_bytes=52 * 1024 * 1024
        ),
    )(
        hidden_in[0],
        norm_gain,
        q_weight[0],
        kv_weight[0],
        kv_cache[0],
        lengths,
    )
    return handed[None], new_kv[None]


def solution(mesh):
    n_sec, n_row, n_col = (mesh.shape[name] for name in ("section", "row", "col"))
    return jax.shard_map(
        functools.partial(shards, n_sec, n_row, n_col),
        mesh=mesh,
        in_specs=(
            P("section", "col", "row"),
            P("section", "row"),
            P("section", "row", "col"),
            P("section", "row", "col"),
            P("section", "col", "row", None, None),
            P("section", "col"),
        ),
        out_specs=(P("section", "col", "row"), P("section", "col", None)),
        check_vma=False,
    )
```

```python
import functools

import jax
import jax.numpy as jnp
from jax import lax
from jax.experimental import pallas as pl
from jax.experimental.pallas import tpu as pltpu
from jax.sharding import PartitionSpec as P

HEAD_DIM = 128
EPSILON = 1e-05
FLOOR = -1e30
MESH = pl.DeviceIdType.MESH
F32 = jnp.float32
BF16 = jnp.bfloat16


def kernel(
    dims,
    hidden_ref,
    gain_hbm,
    qw_ref,
    kvw_ref,
    cache_ref,
    len_hbm,
    handed_ref,
    newkv_hbm,
    newkv_ref,
    weights,
    cache,
    keys,
    values,
    gain_ref,
    len_ref,
    scaled_rows,
    gathered,
    parts,
    arrived,
    summed,
    full,
    outs,
    outs_in,
    stat_rows,
    stat_in,
    squares,
    final,
    weight_sem,
    cache_sem,
    small_sem,
    gather_send,
    gather_recv,
    own_send,
    sum_send,
    sum_recv,
    turn_send,
    turn_recv,
    full_send,
    full_recv,
    out_send,
    out_recv,
    stat_send,
    stat_recv,
    square_send,
    square_recv,
    hand_send,
    hand_recv,
):
    n_sec, n_row, n_col, units, quarter, heads_per, pairs_per, kv_heads = dims
    sec, row, col = lax.axis_index("section"), lax.axis_index("row"), lax.axis_index("col")
    rows, width = hidden_ref.shape
    prompts, positions = cache_ref.shape[0], cache_ref.shape[1]
    samples = rows // prompts
    group = (heads_per * n_col) // kv_heads
    tall = group * samples
    mine = kv_heads // n_row
    tile = quarter * HEAD_DIM
    half = width // 2
    is_end = jnp.logical_or(col == 0, col == n_col - 1)

    mate = row + 1 - 2 * (row % 2)
    across = (row + 2) % 4
    far_peer = (mate + 2) % 4

    def peer(d):
        return lax.rem(row + d, n_row)

    own_loads = [
        pltpu.make_async_copy(
            hidden_ref.at[:, pl.ds(h * half, half)], gathered.at[col, h], small_sem.at[h]
        )
        for h in range(2)
    ]
    gain_load = pltpu.make_async_copy(gain_hbm, gain_ref, small_sem.at[2])
    len_load = pltpu.make_async_copy(len_hbm, len_ref, small_sem.at[3])
    cache_load = pltpu.make_async_copy(cache_ref, cache, cache_sem)
    for load in own_loads + [gain_load, len_load, cache_load]:
        load.start()
    loads, filled = [], 0
    for source in (qw_ref, kvw_ref):
        taken = 0
        while taken < source.shape[1]:
            t, at = filled // tile, filled % tile
            wide = min(source.shape[1] - taken, tile - at)
            loads.append(
                pltpu.make_async_copy(
                    source.at[:, pl.ds(taken, wide)],
                    weights.at[t, :, pl.ds(at, wide)],
                    weight_sem.at[len(loads)],
                )
            )
            taken, filled = taken + wide, filled + wide
    for load in loads:
        load.start()

    barrier = pltpu.get_barrier_semaphore()
    for d in range(1, n_row):
        pl.semaphore_signal(barrier, inc=1, device_id=(sec, peer(d), col), device_id_type=MESH)
    for d in range(1, n_col):
        pl.semaphore_signal(
            barrier, inc=1, device_id=(sec, row, lax.rem(col + d, n_col)), device_id_type=MESH
        )
    pl.semaphore_signal(
        barrier, inc=1, device_id=(lax.rem(sec + n_sec - 1, n_sec), row, col), device_id_type=MESH
    )

    while filled < n_row * tile:
        t, at = filled // tile, filled % tile
        weights[t, :, at:] = jnp.zeros((width, tile - at), BF16)
        filled = (t + 1) * tile
    pl.semaphore_wait(barrier, n_row - 1 + n_col - 1 + 1)

    def gather_copy(block, h, to, send_sem):
        return pltpu.make_async_remote_copy(
            src_ref=gathered.at[block, h],
            dst_ref=gathered.at[block, h],
            send_sem=send_sem.at[h],
            recv_sem=gather_recv.at[block, h],
            device_id=(sec, row, to),
            device_id_type=MESH,
        )

    def own_copy(h, to, send_sem):
        return pltpu.make_async_remote_copy(
            src_ref=hidden_ref.at[:, pl.ds(h * half, half)],
            dst_ref=gathered.at[col, h],
            send_sem=send_sem.at[h],
            recv_sem=gather_recv.at[col, h],
            device_id=(sec, row, to),
            device_id_type=MESH,
        )

    below, above = jnp.maximum(col - 1, 0), jnp.minimum(col + 1, n_col - 1)

    for h in range(2):

        @pl.when(col > 0)
        def _():
            own_copy(h, below, gather_send.at[col]).start()

        @pl.when(col < n_col - 1)
        def _():
            own_copy(h, above, own_send).start()

    for load in own_loads:
        load.wait()
    square = jnp.zeros((rows, 1), F32)
    for h in range(2):
        widened = gathered[col, h].astype(F32)
        square = square + jnp.sum(widened * widened, axis=1, keepdims=True)
    squares[row] = jnp.broadcast_to(square, (rows, HEAD_DIM))

    def square_copy(d):
        return pltpu.make_async_remote_copy(
            src_ref=squares.at[row],
            dst_ref=squares.at[row],
            send_sem=square_send.at[d],
            recv_sem=square_recv.at[row],
            device_id=(sec, peer(d), col),
            device_id_type=MESH,
        )

    for d in range(1, n_row):
        square_copy(d).start()

    slots = 2 * positions
    picked = lax.broadcasted_iota(jnp.int32, (slots, slots), 0)
    offered = lax.broadcasted_iota(jnp.int32, (slots, slots), 1)
    wanted = jnp.where(picked < positions, 2 * picked, 2 * (picked - positions) + 1)
    pick = jnp.where(offered == wanted, 1.0, 0.0).astype(BF16)
    cache_load.wait()
    strip = 2 * HEAD_DIM
    strips = cache_ref.shape[3] // strip

    def split(k, carry):
        p = k // strips
        some = pl.ds(pl.multiple_of((k % strips) * strip, strip), strip)
        both = cache[p, :, :, some].reshape(slots, strip)
        apart = jnp.dot(pick, both, preferred_element_type=F32).astype(BF16)
        keys[p, :, some] = apart[:positions]
        values[p, :, some] = apart[positions:]
        return carry

    shorter = jnp.minimum(col, n_col - 1 - col)
    upward = col < n_col - 1 - col

    def block_at(k):
        away = (k + 1) // 2
        near = jnp.where(k % 2 == 1, col + away, col - away)
        far = jnp.where(upward, col + (k - shorter), col - (k - shorter))
        return jnp.where(k <= 2 * shorter, near, far)

    def pass_on(k, h):
        block = block_at(k)
        gather_copy(block, h, below, gather_send.at[block]).wait_recv()

        @pl.when(block > col)
        def _():
            gather_copy(block, h, below, gather_send.at[block]).start()

        @pl.when(block < col)
        def _():
            gather_copy(block, h, above, gather_send.at[block]).start()

    in_middle = jnp.logical_not(is_end)
    ways = prompts * strips
    for h in range(2):
        lax.fori_loop(h * ways // 2, (h + 1) * ways // 2, split, 0)

        @pl.when(in_middle)
        def _():
            for k in range(1, min(3, n_col)):
                pass_on(k, h)

    def pass_late(h):
        @pl.when(in_middle)
        def _():
            for k in range(3, n_col):
                pass_on(k, h)

    def sum_copy(block, other):
        return pltpu.make_async_remote_copy(
            src_ref=parts.at[block, pl.ds(other * quarter, quarter)],
            dst_ref=arrived.at[block, row],
            send_sem=sum_send.at[block, other],
            recv_sem=sum_recv.at[block, row],
            device_id=(sec, other, col),
            device_id_type=MESH,
        )

    def sum_wait(block, d):
        other = peer(d)
        pltpu.make_async_remote_copy(
            src_ref=arrived.at[block, other],
            dst_ref=arrived.at[block, other],
            send_sem=sum_send.at[block, d],
            recv_sem=sum_recv.at[block, other],
            device_id=(sec, other, col),
            device_id_type=MESH,
        ).wait_recv()

    def full_part(source, part):
        return full.at[pl.ds(source * units + part * quarter, quarter)]

    def full_copy(source, part, to, sem):
        return pltpu.make_async_remote_copy(
            src_ref=full_part(source, part),
            dst_ref=full_part(source, part),
            send_sem=full_send.at[source, sem],
            recv_sem=full_recv.at[source, part],
            device_id=(sec, to, col),
            device_id_type=MESH,
        )

    def spread(source):
        full_copy(source, row, across, 0).start()
        full_copy(source, row, mate, 1).start()

    def relay(source):
        full_copy(source, across, mate, 2).wait_recv()
        full_copy(source, across, mate, 2).start()

    def turn_copy(block):
        return pltpu.make_async_remote_copy(
            src_ref=summed.at[block],
            dst_ref=full_part(col, row),
            send_sem=turn_send.at[block],
            recv_sem=turn_recv.at[col],
            device_id=(sec, row, block),
            device_id_type=MESH,
        )

    def reduce_block(block):
        total = parts[block, pl.ds(row * quarter, quarter)].astype(F32)
        for d in range(1, n_row):
            sum_wait(block, d)
            total = total + arrived[block, peer(d)].astype(F32)
        total = total.astype(BF16)

        @pl.when(block == col)
        def _():
            full[pl.ds(col * units + row * quarter, quarter)] = total
            spread(col)

        @pl.when(block != col)
        def _():
            summed[block] = total
            turn_copy(block).start()

    for load in loads:
        load.wait()

    gain_load.wait()

    def target(j):
        return jnp.where(
            j == 0, across, jnp.where(j == 1, far_peer, jnp.where(j == 2, mate, row))
        )

    def step(first, count, before, between):
        blocks = [block_at(first + i) for i in range(count)]

        @pl.when(is_end)
        def _():
            for i, block in enumerate(blocks):

                @pl.when(first + i > 0)
                def _():
                    for h in range(2):
                        gather_copy(block, h, below, gather_send.at[block]).wait_recv()

        before()
        for i, block in enumerate(blocks):
            for h in range(2):
                raw = gathered[block, h].astype(F32)
                scaled_rows[h, i * rows : (i + 1) * rows] = (
                    raw * gain_ref[:, h * half : (h + 1) * half]
                ).astype(BF16)

        def multiply(j, carry):
            dest = target(j)
            product = jnp.zeros((count * rows, tile), F32)
            for h in range(2):
                product = product + jnp.dot(
                    scaled_rows[h, : count * rows],
                    weights[dest, h * half : (h + 1) * half],
                    preferred_element_type=F32,
                )
            product = product.astype(BF16)
            for i, block in enumerate(blocks):
                for u in range(quarter):
                    parts[block, dest * quarter + u] = product[
                        i * rows : (i + 1) * rows, u * HEAD_DIM : (u + 1) * HEAD_DIM
                    ]

            @pl.when(j < n_row - 1)
            def _():
                for block in blocks:
                    sum_copy(block, dest).start()

            return carry

        lax.fori_loop(0, n_row // 2, multiply, 0)
        between()
        lax.fori_loop(n_row // 2, n_row, multiply, 0)

    step(0, 2, lambda: pass_late(0), lambda: pass_late(1))

    def single(k, carry):
        def between():
            @pl.when(k == 2)
            def _():
                reduce_block(block_at(0))

            reduce_block(block_at(k - 1))

        step(k, 1, lambda: None, between)
        return carry

    lax.fori_loop(2, n_col, single, 0)
    reduce_block(block_at(n_col - 1))

    def forward(k, carry):
        source = block_at(k)
        pltpu.make_async_remote_copy(
            src_ref=full_part(source, row),
            dst_ref=full_part(source, row),
            send_sem=turn_send.at[source],
            recv_sem=turn_recv.at[source],
            device_id=(sec, row, source),
            device_id_type=MESH,
        ).wait_recv()
        spread(source)
        relay(block_at(k - 1))
        return carry

    lax.fori_loop(1, n_col, forward, 0)
    relay(block_at(n_col - 1))

    for d in range(1, n_row):
        other = peer(d)
        pltpu.make_async_remote_copy(
            src_ref=squares.at[other],
            dst_ref=squares.at[other],
            send_sem=square_send.at[d],
            recv_sem=square_recv.at[other],
            device_id=(sec, other, col),
            device_id_type=MESH,
        ).wait_recv()
    square_sum = squares[0]
    for i in range(1, n_row):
        square_sum = square_sum + squares[i]
    len_load.wait()
    scaling = lax.rsqrt(square_sum / (width * n_row) + EPSILON)

    def head_unit(head):
        return (head // heads_per) * units + head % heads_per

    def pair_unit(pair):
        return (pair // pairs_per) * units + heads_per + pair % pairs_per

    def scaled(unit, p):
        some = pl.ds(p * samples, samples)
        factor = scaling[p * samples : (p + 1) * samples]
        return (full[unit, some, :].astype(F32) * factor).astype(BF16)

    def queries(g, p):
        return jnp.concatenate([scaled(head_unit(g * group + i), p) for i in range(group)], axis=0)

    score_scale = HEAD_DIM ** (-0.5)
    lane = lax.broadcasted_iota(jnp.int32, (tall, HEAD_DIM), 1)
    position = row * positions + lax.broadcasted_iota(jnp.int32, (1, positions), 1)
    valid = [position < len_ref[0, p] for p in range(prompts)]

    def attend(heads):
        pairs = [(g, p) for g in heads for p in range(prompts)]

        def some(g):
            return pl.ds(pl.multiple_of(g * HEAD_DIM, HEAD_DIM), HEAD_DIM)

        scores = [
            lax.dot_general(
                queries(g, p),
                keys[p, :, some(g)],
                (((1,), (1,)), ((), ())),
                preferred_element_type=F32,
            )
            for g, p in pairs
        ]
        scores = [
            jnp.where(valid[p], score * score_scale, FLOOR)
            for (g, p), score in zip(pairs, scores)
        ]
        tops = [jnp.max(score, axis=1, keepdims=True) for score in scores]
        raised = [
            jnp.where(valid[p], jnp.exp(score - top), 0.0)
            for (g, p), score, top in zip(pairs, scores, tops)
        ]
        totals = [jnp.sum(weight, axis=1, keepdims=True) for weight in raised]
        products = [
            jnp.dot(weight.astype(BF16), values[p, :, some(g)], preferred_element_type=F32)
            for (g, p), weight in zip(pairs, raised)
        ]
        for (g, p), product in zip(pairs, products):
            outs[g, p] = product.astype(BF16)
        for i, g in enumerate(heads):
            both = jnp.zeros((tall, HEAD_DIM), F32)
            for p in range(prompts):
                both = jnp.where(lane == 2 * p, tops[i * prompts + p], both)
                both = jnp.where(lane == 2 * p + 1, totals[i * prompts + p], both)
            stat_rows[g] = both.T[:8]

    def out_copy(dest):
        return pltpu.make_async_remote_copy(
            src_ref=outs.at[pl.ds(dest * mine, mine)],
            dst_ref=outs_in.at[row],
            send_sem=out_send.at[dest],
            recv_sem=out_recv.at[row],
            device_id=(sec, dest, col),
            device_id_type=MESH,
        )

    chunk_heads = max(1, heads_per // group)
    chunk_cols = max(1, group // heads_per)
    chunks = kv_heads // chunk_heads
    by_dest = chunks == n_row and chunk_heads == mine

    def stat_copy(dest):
        return pltpu.make_async_remote_copy(
            src_ref=stat_rows.at[pl.ds(dest * mine, mine)],
            dst_ref=stat_in.at[row],
            send_sem=stat_send.at[dest],
            recv_sem=stat_recv.at[row],
            device_id=(sec, dest, col),
            device_id_type=MESH,
        )

    def chunk(k, carry):
        j = k
        if by_dest:
            j = target(k)
        for i in range(chunk_cols):
            source = j * chunk_cols + i
            full_copy(source, mate, mate, 1).wait_recv()
            full_copy(source, far_peer, mate, 2).wait_recv()
        attend([j * chunk_heads + i for i in range(chunk_heads)])
        last = j * chunk_heads + chunk_heads - 1
        dest = last // mine

        @pl.when(jnp.logical_and(last % mine == mine - 1, dest != row))
        def _():
            out_copy(dest).start()
            stat_copy(dest).start()

        return carry

    lax.fori_loop(0, chunks, chunk, 0)

    outs_in[row] = outs[pl.ds(row * mine, mine)]
    stat_in[row] = stat_rows[pl.ds(row * mine, mine)]

    for pair in range(2 * kv_heads):
        newkv_ref[:, pair * HEAD_DIM : (pair + 1) * HEAD_DIM] = (
            full[pair_unit(pair)].astype(F32) * scaling
        ).astype(BF16)

    newkv_store = pltpu.make_async_copy(newkv_ref, newkv_hbm, small_sem.at[4])
    newkv_store.start()

    def own_part(g, p):
        new_key = jnp.concatenate([scaled(pair_unit(g), p)] * group, axis=0)
        product = queries(g, p).astype(F32) * new_key.astype(F32)
        return jnp.sum(product, axis=1, keepdims=True) * score_scale

    own_scores = [[own_part(row * mine + i, p) for p in range(prompts)] for i in range(mine)]

    for d in range(1, n_row):
        other = peer(d)
        pltpu.make_async_remote_copy(
            src_ref=stat_in.at[other],
            dst_ref=stat_in.at[other],
            send_sem=stat_send.at[other],
            recv_sem=stat_recv.at[other],
            device_id=(sec, other, col),
            device_id_type=MESH,
        ).wait_recv()
        pltpu.make_async_remote_copy(
            src_ref=outs_in.at[other],
            dst_ref=outs_in.at[other],
            send_sem=out_send.at[other],
            recv_sem=out_recv.at[other],
            device_id=(sec, other, col),
            device_id_type=MESH,
        ).wait_recv()

    lines = stat_in[...].reshape(n_row * mine * 8, tall)
    stats = jnp.concatenate([lines, jnp.zeros((HEAD_DIM - n_row * mine * 8, tall), F32)], axis=0).T
    span = group * HEAD_DIM

    def hand_copy(i):
        return pltpu.make_async_remote_copy(
            src_ref=final.at[:, pl.ds(i * span, span)],
            dst_ref=handed_ref.at[:, pl.ds(i * span, span)],
            send_sem=hand_send.at[i],
            recv_sem=hand_recv.at[i],
            device_id=(lax.rem(sec + 1, n_sec), row, col),
            device_id_type=MESH,
        )

    for i in range(mine):
        g = row * mine + i
        for p in range(prompts):
            new_value = jnp.concatenate([scaled(pair_unit(kv_heads + g), p)] * group, axis=0)
            own = own_scores[i][p]
            top = own
            tops, totals = [], []
            for s in range(n_row):
                at = (s * mine + i) * 8 + 2 * p
                tops.append(stats[:, at : at + 1])
                totals.append(stats[:, at + 1 : at + 2])
                top = jnp.maximum(top, tops[-1])
            own_weight = jnp.exp(own - top)
            total = own_weight
            value = own_weight.astype(BF16).astype(F32) * new_value.astype(F32)
            for s in range(n_row):
                keep = jnp.exp(tops[s] - top)
                total = total + keep * totals[s]
                value = value + keep * outs_in[s, i, p].astype(F32)
            done = (value / total).astype(BF16)
            for h in range(group):
                first = (i * group + h) * HEAD_DIM
                final[p * samples : (p + 1) * samples, first : first + HEAD_DIM] = done[
                    h * samples : (h + 1) * samples
                ]
        hand_copy(i).start()

    for h in range(2):

        @pl.when(col > 0)
        def _():
            own_copy(h, below, gather_send.at[col]).wait_send()

        @pl.when(col < n_col - 1)
        def _():
            own_copy(h, above, own_send).wait_send()

    def drain(k, carry):
        block = block_at(k)

        @pl.when(jnp.logical_and(block != col, jnp.logical_not(is_end)))
        def _():
            for h in range(2):
                gather_copy(block, h, below, gather_send.at[block]).wait_send()

        @pl.when(block != col)
        def _():
            turn_copy(block).wait_send()

        for d in range(1, n_row):
            sum_copy(block, peer(d)).wait_send()
        full_copy(block, row, across, 0).wait_send()
        full_copy(block, row, mate, 1).wait_send()
        full_copy(block, across, mate, 2).wait_send()
        return carry

    lax.fori_loop(0, n_col, drain, 0)
    for d in range(1, n_row):
        square_copy(d).wait_send()
        stat_copy(peer(d)).wait_send()
        out_copy(peer(d)).wait_send()
    newkv_store.wait()
    for i in range(mine):
        hand_copy(i).wait()


def copy_both(first_ref, second_ref, first_out, second_out, sem):
    copies = [
        pltpu.make_async_copy(first_ref, first_out, sem.at[0]),
        pltpu.make_async_copy(second_ref, second_out, sem.at[1]),
    ]
    for copy in copies:
        copy.start()
    for copy in copies:
        copy.wait()


def shards(n_sec, n_row, n_col, hidden_in, norm_gain, q_weight, kv_weight, kv_cache, lengths):
    _, rows, width = hidden_in.shape
    _, prompts, positions, _, cache_width = kv_cache.shape
    kv_heads = cache_width // HEAD_DIM
    heads_per = q_weight.shape[2] // HEAD_DIM
    pairs_per = kv_weight.shape[2] // HEAD_DIM
    units = -(-(heads_per + pairs_per) // 4) * 4
    quarter = units // n_row
    group = heads_per * n_col // kv_heads
    tall = group * (rows // prompts)
    mine = kv_heads // n_row
    dims = (n_sec, n_row, n_col, units, quarter, heads_per, pairs_per, kv_heads)
    dma = pltpu.SemaphoreType.DMA
    handed, new_kv = pl.pallas_call(
        functools.partial(kernel, dims),
        out_shape=(
            jax.ShapeDtypeStruct((rows, heads_per * n_col // n_row * HEAD_DIM), BF16),
            jax.ShapeDtypeStruct((rows, 2 * cache_width), BF16),
        ),
        in_specs=[pl.BlockSpec(memory_space=pltpu.HBM)] * 6,
        out_specs=[pl.BlockSpec(memory_space=pltpu.HBM)] * 2,
        scratch_shapes=[
            pltpu.VMEM((rows, 2 * cache_width), BF16),
            pltpu.VMEM((n_row, width, quarter * HEAD_DIM), BF16),
            pltpu.VMEM((prompts, positions, 2, cache_width), BF16),
            pltpu.VMEM((prompts, positions, cache_width), BF16),
            pltpu.VMEM((prompts, positions, cache_width), BF16),
            pltpu.VMEM((1, width), F32),
            pltpu.SMEM((1, prompts), jnp.int32),
            pltpu.VMEM((2, 2 * rows, width // 2), BF16),
            pltpu.VMEM((n_col, 2, rows, width // 2), BF16),
            pltpu.VMEM((n_col, units, rows, HEAD_DIM), BF16),
            pltpu.VMEM((n_col, n_row, quarter, rows, HEAD_DIM), BF16),
            pltpu.VMEM((n_col, quarter, rows, HEAD_DIM), BF16),
            pltpu.VMEM((n_col * units, rows, HEAD_DIM), BF16),
            pltpu.VMEM((kv_heads, prompts, tall, HEAD_DIM), BF16),
            pltpu.VMEM((n_row, mine, prompts, tall, HEAD_DIM), BF16),
            pltpu.VMEM((kv_heads, 8, tall), F32),
            pltpu.VMEM((n_row, mine, 8, tall), F32),
            pltpu.VMEM((n_row, rows, HEAD_DIM), F32),
            pltpu.VMEM((rows, heads_per * n_col // n_row * HEAD_DIM), BF16),
            dma((2 * n_row + 2,)),
            dma,
            dma((5,)),
            dma((n_col, 2)),
            dma((n_col, 2)),
            dma((2,)),
            dma((n_col, n_row)),
            dma((n_col, n_row)),
            dma((n_col,)),
            dma((n_col,)),
            dma((n_col, n_row)),
            dma((n_col, n_row)),
            dma((n_row,)),
            dma((n_row,)),
            dma((n_row,)),
            dma((n_row,)),
            dma((n_row,)),
            dma((n_row,)),
            dma((mine,)),
            dma((mine,)),
        ],
        compiler_params=pltpu.CompilerParams(
            collective_id=0, has_side_effects=True, vmem_limit_bytes=60 * 1024 * 1024
        ),
    )(
        hidden_in[0],
        norm_gain,
        q_weight[0],
        kv_weight[0],
        kv_cache[0],
        lengths,
    )
    outputs = (handed, new_kv)
    handed, new_kv = pl.pallas_call(
        copy_both,
        out_shape=tuple(jax.ShapeDtypeStruct(x.shape, x.dtype) for x in outputs),
        in_specs=[pl.BlockSpec(memory_space=pl.ANY)] * 2,
        out_specs=[pl.BlockSpec(memory_space=pltpu.HBM)] * 2,
        scratch_shapes=[dma((2,))],
    )(*outputs)
    return handed[None], new_kv[None]


def solution(mesh):
    n_sec, n_row, n_col = (mesh.shape[name] for name in ("section", "row", "col"))
    return jax.shard_map(
        functools.partial(shards, n_sec, n_row, n_col),
        mesh=mesh,
        in_specs=(
            P("section", "col", "row"),
            P("section", "row"),
            P("section", "row", "col"),
            P("section", "row", "col"),
            P("section", "col", "row", None, None),
            P("section", "col"),
        ),
        out_specs=(P("section", "col", "row"), P("section", "col", None)),
        check_vma=False,
    )
```

```python
import functools

import jax
import jax.numpy as jnp
from jax import lax
from jax.experimental import pallas as pl
from jax.experimental.pallas import tpu as pltpu
from jax.sharding import PartitionSpec as P

HEAD_DIM = 128
EPSILON = 1e-05
FLOOR = -1e30
MESH = pl.DeviceIdType.MESH
F32 = jnp.float32
BF16 = jnp.bfloat16


def kernel(
    dims,
    hidden_ref,
    gain_hbm,
    qw_ref,
    kvw_ref,
    cache_ref,
    len_hbm,
    handed_ref,
    newkv_ref,
    weights,
    cache,
    keys,
    values,
    gain_ref,
    len_ref,
    scaled_rows,
    gathered,
    parts,
    arrived,
    summed,
    full,
    outs,
    outs_in,
    stat_rows,
    stat_in,
    squares,
    final,
    weight_sem,
    cache_sem,
    small_sem,
    gather_send,
    gather_recv,
    own_send,
    sum_send,
    sum_recv,
    turn_send,
    turn_recv,
    full_send,
    full_recv,
    out_send,
    out_recv,
    stat_send,
    stat_recv,
    square_send,
    square_recv,
    hand_send,
    hand_recv,
):
    n_sec, n_row, n_col, units, quarter, heads_per, pairs_per, kv_heads = dims
    sec, row, col = lax.axis_index("section"), lax.axis_index("row"), lax.axis_index("col")
    rows, width = hidden_ref.shape
    prompts, positions = cache_ref.shape[0], cache_ref.shape[1]
    samples = rows // prompts
    group = (heads_per * n_col) // kv_heads
    tall = group * samples
    mine = kv_heads // n_row
    tile = quarter * HEAD_DIM
    half = width // 2
    is_end = jnp.logical_or(col == 0, col == n_col - 1)

    mate = row + 1 - 2 * (row % 2)
    across = (row + 2) % 4
    far_peer = (mate + 2) % 4

    def peer(d):
        return lax.rem(row + d, n_row)

    own_loads = [
        pltpu.make_async_copy(
            hidden_ref.at[:, pl.ds(h * half, half)], gathered.at[col, h], small_sem.at[h]
        )
        for h in range(2)
    ]
    gain_load = pltpu.make_async_copy(gain_hbm, gain_ref, small_sem.at[2])
    len_load = pltpu.make_async_copy(len_hbm, len_ref, small_sem.at[3])
    cache_load = pltpu.make_async_copy(cache_ref, cache, cache_sem)
    for load in own_loads + [gain_load, len_load, cache_load]:
        load.start()
    loads, filled = [], 0
    for source in (qw_ref, kvw_ref):
        taken = 0
        while taken < source.shape[1]:
            t, at = filled // tile, filled % tile
            wide = min(source.shape[1] - taken, tile - at)
            loads.append(
                pltpu.make_async_copy(
                    source.at[:, pl.ds(taken, wide)],
                    weights.at[t, :, pl.ds(at, wide)],
                    weight_sem.at[len(loads)],
                )
            )
            taken, filled = taken + wide, filled + wide
    for load in loads:
        load.start()

    barrier = pltpu.get_barrier_semaphore()
    for d in range(1, n_row):
        pl.semaphore_signal(barrier, inc=1, device_id=(sec, peer(d), col), device_id_type=MESH)
    for d in range(1, n_col):
        pl.semaphore_signal(
            barrier, inc=1, device_id=(sec, row, lax.rem(col + d, n_col)), device_id_type=MESH
        )
    pl.semaphore_signal(
        barrier, inc=1, device_id=(lax.rem(sec + n_sec - 1, n_sec), row, col), device_id_type=MESH
    )

    while filled < n_row * tile:
        t, at = filled // tile, filled % tile
        weights[t, :, at:] = jnp.zeros((width, tile - at), BF16)
        filled = (t + 1) * tile
    pl.semaphore_wait(barrier, n_row - 1 + n_col - 1 + 1)

    def gather_copy(block, h, to, send_sem):
        return pltpu.make_async_remote_copy(
            src_ref=gathered.at[block, h],
            dst_ref=gathered.at[block, h],
            send_sem=send_sem.at[h],
            recv_sem=gather_recv.at[block, h],
            device_id=(sec, row, to),
            device_id_type=MESH,
        )

    def own_copy(h, to, send_sem):
        return pltpu.make_async_remote_copy(
            src_ref=hidden_ref.at[:, pl.ds(h * half, half)],
            dst_ref=gathered.at[col, h],
            send_sem=send_sem.at[h],
            recv_sem=gather_recv.at[col, h],
            device_id=(sec, row, to),
            device_id_type=MESH,
        )

    below, above = jnp.maximum(col - 1, 0), jnp.minimum(col + 1, n_col - 1)

    for h in range(2):

        @pl.when(col > 0)
        def _():
            own_copy(h, below, gather_send.at[col]).start()

        @pl.when(col < n_col - 1)
        def _():
            own_copy(h, above, own_send).start()

    for load in own_loads:
        load.wait()
    square = jnp.zeros((rows, 1), F32)
    for h in range(2):
        widened = gathered[col, h].astype(F32)
        square = square + jnp.sum(widened * widened, axis=1, keepdims=True)
    squares[row] = jnp.broadcast_to(square, (rows, HEAD_DIM))

    def square_copy(d):
        return pltpu.make_async_remote_copy(
            src_ref=squares.at[row],
            dst_ref=squares.at[row],
            send_sem=square_send.at[d],
            recv_sem=square_recv.at[row],
            device_id=(sec, peer(d), col),
            device_id_type=MESH,
        )

    for d in range(1, n_row):
        square_copy(d).start()

    slots = 2 * positions
    picked = lax.broadcasted_iota(jnp.int32, (slots, slots), 0)
    offered = lax.broadcasted_iota(jnp.int32, (slots, slots), 1)
    wanted = jnp.where(picked < positions, 2 * picked, 2 * (picked - positions) + 1)
    pick = jnp.where(offered == wanted, 1.0, 0.0).astype(BF16)
    cache_load.wait()
    strip = 2 * HEAD_DIM
    strips = cache_ref.shape[3] // strip

    def split(k, carry):
        p = k // strips
        some = pl.ds(pl.multiple_of((k % strips) * strip, strip), strip)
        both = cache[p, :, :, some].reshape(slots, strip)
        apart = jnp.dot(pick, both, preferred_element_type=F32).astype(BF16)
        keys[p, :, some] = apart[:positions]
        values[p, :, some] = apart[positions:]
        return carry

    shorter = jnp.minimum(col, n_col - 1 - col)
    upward = col < n_col - 1 - col

    def block_at(k):
        away = (k + 1) // 2
        near = jnp.where(k % 2 == 1, col + away, col - away)
        far = jnp.where(upward, col + (k - shorter), col - (k - shorter))
        return jnp.where(k <= 2 * shorter, near, far)

    def pass_on(k, h):
        block = block_at(k)
        gather_copy(block, h, below, gather_send.at[block]).wait_recv()

        @pl.when(block > col)
        def _():
            gather_copy(block, h, below, gather_send.at[block]).start()

        @pl.when(block < col)
        def _():
            gather_copy(block, h, above, gather_send.at[block]).start()

    in_middle = jnp.logical_not(is_end)
    ways = prompts * strips
    for h in range(2):
        lax.fori_loop(h * ways // 2, (h + 1) * ways // 2, split, 0)

        @pl.when(in_middle)
        def _():
            for k in range(1, min(3, n_col)):
                pass_on(k, h)

    def pass_late(h):
        @pl.when(in_middle)
        def _():
            for k in range(3, n_col):
                pass_on(k, h)

    def sum_copy(block, other):
        return pltpu.make_async_remote_copy(
            src_ref=parts.at[block, pl.ds(other * quarter, quarter)],
            dst_ref=arrived.at[block, row],
            send_sem=sum_send.at[block, other],
            recv_sem=sum_recv.at[block, row],
            device_id=(sec, other, col),
            device_id_type=MESH,
        )

    def sum_wait(block, d):
        other = peer(d)
        pltpu.make_async_remote_copy(
            src_ref=arrived.at[block, other],
            dst_ref=arrived.at[block, other],
            send_sem=sum_send.at[block, d],
            recv_sem=sum_recv.at[block, other],
            device_id=(sec, other, col),
            device_id_type=MESH,
        ).wait_recv()

    def full_part(source, part):
        return full.at[pl.ds(source * units + part * quarter, quarter)]

    def full_copy(source, part, to, sem):
        return pltpu.make_async_remote_copy(
            src_ref=full_part(source, part),
            dst_ref=full_part(source, part),
            send_sem=full_send.at[source, sem],
            recv_sem=full_recv.at[source, part],
            device_id=(sec, to, col),
            device_id_type=MESH,
        )

    def spread(source):
        full_copy(source, row, across, 0).start()
        full_copy(source, row, mate, 1).start()

    def relay(source):
        full_copy(source, across, mate, 2).wait_recv()
        full_copy(source, across, mate, 2).start()

    def turn_copy(block):
        return pltpu.make_async_remote_copy(
            src_ref=summed.at[block],
            dst_ref=full_part(col, row),
            send_sem=turn_send.at[block],
            recv_sem=turn_recv.at[col],
            device_id=(sec, row, block),
            device_id_type=MESH,
        )

    def reduce_block(block):
        total = parts[block, pl.ds(row * quarter, quarter)].astype(F32)
        for d in range(1, n_row):
            sum_wait(block, d)
            total = total + arrived[block, peer(d)].astype(F32)
        total = total.astype(BF16)

        @pl.when(block == col)
        def _():
            full[pl.ds(col * units + row * quarter, quarter)] = total
            spread(col)

        @pl.when(block != col)
        def _():
            summed[block] = total
            turn_copy(block).start()

    for load in loads:
        load.wait()

    gain_load.wait()

    def target(j):
        return jnp.where(
            j == 0, across, jnp.where(j == 1, far_peer, jnp.where(j == 2, mate, row))
        )

    def step(first, count, before, between):
        blocks = [block_at(first + i) for i in range(count)]

        @pl.when(is_end)
        def _():
            for i, block in enumerate(blocks):

                @pl.when(first + i > 0)
                def _():
                    for h in range(2):
                        gather_copy(block, h, below, gather_send.at[block]).wait_recv()

        before()
        for i, block in enumerate(blocks):
            for h in range(2):
                raw = gathered[block, h].astype(F32)
                scaled_rows[h, i * rows : (i + 1) * rows] = (
                    raw * gain_ref[:, h * half : (h + 1) * half]
                ).astype(BF16)

        def multiply(j, carry):
            dest = target(j)
            product = jnp.zeros((count * rows, tile), F32)
            for h in range(2):
                product = product + jnp.dot(
                    scaled_rows[h, : count * rows],
                    weights[dest, h * half : (h + 1) * half],
                    preferred_element_type=F32,
                )
            product = product.astype(BF16)
            for i, block in enumerate(blocks):
                for u in range(quarter):
                    parts[block, dest * quarter + u] = product[
                        i * rows : (i + 1) * rows, u * HEAD_DIM : (u + 1) * HEAD_DIM
                    ]

            @pl.when(j < n_row - 1)
            def _():
                for block in blocks:
                    sum_copy(block, dest).start()

            return carry

        lax.fori_loop(0, n_row // 2, multiply, 0)
        between()
        lax.fori_loop(n_row // 2, n_row, multiply, 0)

    step(0, 2, lambda: pass_late(0), lambda: pass_late(1))

    def single(k, carry):
        def between():
            @pl.when(k == 2)
            def _():
                reduce_block(block_at(0))

            reduce_block(block_at(k - 1))

        step(k, 1, lambda: None, between)
        return carry

    lax.fori_loop(2, n_col, single, 0)
    reduce_block(block_at(n_col - 1))

    relay(col)

    for d in range(1, n_row):
        other = peer(d)
        pltpu.make_async_remote_copy(
            src_ref=squares.at[other],
            dst_ref=squares.at[other],
            send_sem=square_send.at[d],
            recv_sem=square_recv.at[other],
            device_id=(sec, other, col),
            device_id_type=MESH,
        ).wait_recv()
    square_sum = squares[0]
    for i in range(1, n_row):
        square_sum = square_sum + squares[i]
    len_load.wait()
    scaling = lax.rsqrt(square_sum / (width * n_row) + EPSILON)

    def head_unit(head):
        return (head // heads_per) * units + head % heads_per

    def pair_unit(pair):
        return (pair // pairs_per) * units + heads_per + pair % pairs_per

    def scaled(unit, p):
        some = pl.ds(p * samples, samples)
        factor = scaling[p * samples : (p + 1) * samples]
        return (full[unit, some, :].astype(F32) * factor).astype(BF16)

    def queries(g, p):
        return jnp.concatenate([scaled(head_unit(g * group + i), p) for i in range(group)], axis=0)

    score_scale = HEAD_DIM ** (-0.5)
    lane = lax.broadcasted_iota(jnp.int32, (tall, HEAD_DIM), 1)
    position = row * positions + lax.broadcasted_iota(jnp.int32, (1, positions), 1)
    valid = [position < len_ref[0, p] for p in range(prompts)]

    def attend(heads):
        pairs = [(g, p) for g in heads for p in range(prompts)]

        def some(g):
            return pl.ds(pl.multiple_of(g * HEAD_DIM, HEAD_DIM), HEAD_DIM)

        scores = [
            lax.dot_general(
                queries(g, p),
                keys[p, :, some(g)],
                (((1,), (1,)), ((), ())),
                preferred_element_type=F32,
            )
            for g, p in pairs
        ]
        scores = [
            jnp.where(valid[p], score * score_scale, FLOOR)
            for (g, p), score in zip(pairs, scores)
        ]
        tops = [jnp.max(score, axis=1, keepdims=True) for score in scores]
        raised = [
            jnp.where(valid[p], jnp.exp(score - top), 0.0)
            for (g, p), score, top in zip(pairs, scores, tops)
        ]
        totals = [jnp.sum(weight, axis=1, keepdims=True) for weight in raised]
        products = [
            jnp.dot(weight.astype(BF16), values[p, :, some(g)], preferred_element_type=F32)
            for (g, p), weight in zip(pairs, raised)
        ]
        for (g, p), product in zip(pairs, products):
            outs[g, p] = product.astype(BF16)
        for i, g in enumerate(heads):
            both = jnp.zeros((tall, HEAD_DIM), F32)
            for p in range(prompts):
                both = jnp.where(lane == 2 * p, tops[i * prompts + p], both)
                both = jnp.where(lane == 2 * p + 1, totals[i * prompts + p], both)
            stat_rows[g] = both.T[:8]

    def out_copy(dest):
        return pltpu.make_async_remote_copy(
            src_ref=outs.at[pl.ds(dest * mine, mine)],
            dst_ref=outs_in.at[row],
            send_sem=out_send.at[dest],
            recv_sem=out_recv.at[row],
            device_id=(sec, dest, col),
            device_id_type=MESH,
        )

    chunk_heads = max(1, heads_per // group)
    chunk_cols = max(1, group // heads_per)
    chunks = kv_heads // chunk_heads
    by_dest = chunks == n_row and chunk_heads == mine and chunks == n_col
    col_turn = jnp.where(
        col == across, 0, jnp.where(col == far_peer, 1, jnp.where(col == mate, 2, 3))
    )

    def stat_copy(dest):
        return pltpu.make_async_remote_copy(
            src_ref=stat_rows.at[pl.ds(dest * mine, mine)],
            dst_ref=stat_in.at[row],
            send_sem=stat_send.at[dest],
            recv_sem=stat_recv.at[row],
            device_id=(sec, dest, col),
            device_id_type=MESH,
        )

    def chunk(k, carry):
        j = k
        if by_dest:
            j = jnp.where(k == 0, col, target(jnp.where(k > col_turn, k, k - 1)))
        for i in range(chunk_cols):
            source = j * chunk_cols + i
            full_copy(source, mate, mate, 1).wait_recv()
            full_copy(source, far_peer, mate, 2).wait_recv()
        attend([j * chunk_heads + i for i in range(chunk_heads)])
        last = j * chunk_heads + chunk_heads - 1
        dest = last // mine

        @pl.when(jnp.logical_and(last % mine == mine - 1, dest != row))
        def _():
            out_copy(dest).start()
            stat_copy(dest).start()

        return carry

    early = 1 if by_dest else 0
    lax.fori_loop(0, early, chunk, 0)

    def forward(k, carry):
        source = block_at(k)
        pltpu.make_async_remote_copy(
            src_ref=full_part(source, row),
            dst_ref=full_part(source, row),
            send_sem=turn_send.at[source],
            recv_sem=turn_recv.at[source],
            device_id=(sec, row, source),
            device_id_type=MESH,
        ).wait_recv()
        spread(source)

        @pl.when(k > 1)
        def _():
            relay(block_at(k - 1))

        return carry

    lax.fori_loop(1, n_col, forward, 0)

    @pl.when(n_col > 1)
    def _():
        relay(block_at(n_col - 1))
    lax.fori_loop(early, chunks, chunk, 0)

    outs_in[row] = outs[pl.ds(row * mine, mine)]
    stat_in[row] = stat_rows[pl.ds(row * mine, mine)]

    for pair in range(2 * kv_heads):
        newkv_ref[:, pair * HEAD_DIM : (pair + 1) * HEAD_DIM] = (
            full[pair_unit(pair)].astype(F32) * scaling
        ).astype(BF16)

    def own_part(g, p):
        new_key = jnp.concatenate([scaled(pair_unit(g), p)] * group, axis=0)
        product = queries(g, p).astype(F32) * new_key.astype(F32)
        return jnp.sum(product, axis=1, keepdims=True) * score_scale

    own_scores = [[own_part(row * mine + i, p) for p in range(prompts)] for i in range(mine)]

    for d in range(1, n_row):
        other = peer(d)
        pltpu.make_async_remote_copy(
            src_ref=stat_in.at[other],
            dst_ref=stat_in.at[other],
            send_sem=stat_send.at[other],
            recv_sem=stat_recv.at[other],
            device_id=(sec, other, col),
            device_id_type=MESH,
        ).wait_recv()
        pltpu.make_async_remote_copy(
            src_ref=outs_in.at[other],
            dst_ref=outs_in.at[other],
            send_sem=out_send.at[other],
            recv_sem=out_recv.at[other],
            device_id=(sec, other, col),
            device_id_type=MESH,
        ).wait_recv()

    lines = stat_in[...].reshape(n_row * mine * 8, tall)
    stats = jnp.concatenate([lines, jnp.zeros((HEAD_DIM - n_row * mine * 8, tall), F32)], axis=0).T
    span = group * HEAD_DIM

    def hand_copy(i, p):
        piece = (pl.ds(p * samples, samples), pl.ds(i * span, span))
        return pltpu.make_async_remote_copy(
            src_ref=final.at[piece],
            dst_ref=handed_ref.at[piece],
            send_sem=hand_send.at[i, p],
            recv_sem=hand_recv.at[i, p],
            device_id=(lax.rem(sec + 1, n_sec), row, col),
            device_id_type=MESH,
        )

    for i in range(mine):
        g = row * mine + i
        for p in range(prompts):
            new_value = jnp.concatenate([scaled(pair_unit(kv_heads + g), p)] * group, axis=0)
            own = own_scores[i][p]
            top = own
            tops, totals = [], []
            for s in range(n_row):
                at = (s * mine + i) * 8 + 2 * p
                tops.append(stats[:, at : at + 1])
                totals.append(stats[:, at + 1 : at + 2])
                top = jnp.maximum(top, tops[-1])
            own_weight = jnp.exp(own - top)
            total = own_weight
            value = own_weight.astype(BF16).astype(F32) * new_value.astype(F32)
            for s in range(n_row):
                keep = jnp.exp(tops[s] - top)
                total = total + keep * totals[s]
                value = value + keep * outs_in[s, i, p].astype(F32)
            done = (value / total).astype(BF16)
            for h in range(group):
                first = (i * group + h) * HEAD_DIM
                final[p * samples : (p + 1) * samples, first : first + HEAD_DIM] = done[
                    h * samples : (h + 1) * samples
                ]
            hand_copy(i, p).start()

    for h in range(2):

        @pl.when(col > 0)
        def _():
            own_copy(h, below, gather_send.at[col]).wait_send()

        @pl.when(col < n_col - 1)
        def _():
            own_copy(h, above, own_send).wait_send()

    def drain(k, carry):
        block = block_at(k)

        @pl.when(jnp.logical_and(block != col, jnp.logical_not(is_end)))
        def _():
            for h in range(2):
                gather_copy(block, h, below, gather_send.at[block]).wait_send()

        @pl.when(block != col)
        def _():
            turn_copy(block).wait_send()

        for d in range(1, n_row):
            sum_copy(block, peer(d)).wait_send()
        full_copy(block, row, across, 0).wait_send()
        full_copy(block, row, mate, 1).wait_send()
        full_copy(block, across, mate, 2).wait_send()
        return carry

    lax.fori_loop(0, n_col, drain, 0)
    for d in range(1, n_row):
        square_copy(d).wait_send()
        stat_copy(peer(d)).wait_send()
        out_copy(peer(d)).wait_send()
    for i in range(mine):
        for p in range(prompts):
            hand_copy(i, p).wait()


def shards(n_sec, n_row, n_col, hidden_in, norm_gain, q_weight, kv_weight, kv_cache, lengths):
    _, rows, width = hidden_in.shape
    _, prompts, positions, _, cache_width = kv_cache.shape
    kv_heads = cache_width // HEAD_DIM
    heads_per = q_weight.shape[2] // HEAD_DIM
    pairs_per = kv_weight.shape[2] // HEAD_DIM
    units = -(-(heads_per + pairs_per) // 4) * 4
    quarter = units // n_row
    group = heads_per * n_col // kv_heads
    tall = group * (rows // prompts)
    mine = kv_heads // n_row
    dims = (n_sec, n_row, n_col, units, quarter, heads_per, pairs_per, kv_heads)
    dma = pltpu.SemaphoreType.DMA
    handed, new_kv = pl.pallas_call(
        functools.partial(kernel, dims),
        out_shape=(
            jax.ShapeDtypeStruct((rows, heads_per * n_col // n_row * HEAD_DIM), BF16),
            jax.ShapeDtypeStruct((rows, 2 * cache_width), BF16),
        ),
        in_specs=[pl.BlockSpec(memory_space=pltpu.HBM)] * 6,
        out_specs=[pl.BlockSpec(memory_space=pltpu.VMEM)] * 2,
        scratch_shapes=[
            pltpu.VMEM((n_row, width, quarter * HEAD_DIM), BF16),
            pltpu.VMEM((prompts, positions, 2, cache_width), BF16),
            pltpu.VMEM((prompts, positions, cache_width), BF16),
            pltpu.VMEM((prompts, positions, cache_width), BF16),
            pltpu.VMEM((1, width), F32),
            pltpu.SMEM((1, prompts), jnp.int32),
            pltpu.VMEM((2, 2 * rows, width // 2), BF16),
            pltpu.VMEM((n_col, 2, rows, width // 2), BF16),
            pltpu.VMEM((n_col, units, rows, HEAD_DIM), BF16),
            pltpu.VMEM((n_col, n_row, quarter, rows, HEAD_DIM), BF16),
            pltpu.VMEM((n_col, quarter, rows, HEAD_DIM), BF16),
            pltpu.VMEM((n_col * units, rows, HEAD_DIM), BF16),
            pltpu.VMEM((kv_heads, prompts, tall, HEAD_DIM), BF16),
            pltpu.VMEM((n_row, mine, prompts, tall, HEAD_DIM), BF16),
            pltpu.VMEM((kv_heads, 8, tall), F32),
            pltpu.VMEM((n_row, mine, 8, tall), F32),
            pltpu.VMEM((n_row, rows, HEAD_DIM), F32),
            pltpu.VMEM((rows, heads_per * n_col // n_row * HEAD_DIM), BF16),
            dma((2 * n_row + 2,)),
            dma,
            dma((4,)),
            dma((n_col, 2)),
            dma((n_col, 2)),
            dma((2,)),
            dma((n_col, n_row)),
            dma((n_col, n_row)),
            dma((n_col,)),
            dma((n_col,)),
            dma((n_col, n_row)),
            dma((n_col, n_row)),
            dma((n_row,)),
            dma((n_row,)),
            dma((n_row,)),
            dma((n_row,)),
            dma((n_row,)),
            dma((n_row,)),
            dma((mine, prompts)),
            dma((mine, prompts)),
        ],
        compiler_params=pltpu.CompilerParams(
            collective_id=0, has_side_effects=True, vmem_limit_bytes=54912 * 1024
        ),
    )(
        hidden_in[0],
        norm_gain,
        q_weight[0],
        kv_weight[0],
        kv_cache[0],
        lengths,
    )
    return handed[None], new_kv[None]


def solution(mesh):
    n_sec, n_row, n_col = (mesh.shape[name] for name in ("section", "row", "col"))
    return jax.shard_map(
        functools.partial(shards, n_sec, n_row, n_col),
        mesh=mesh,
        in_specs=(
            P("section", "col", "row"),
            P("section", "row"),
            P("section", "row", "col"),
            P("section", "row", "col"),
            P("section", "col", "row", None, None),
            P("section", "col"),
        ),
        out_specs=(P("section", "col", "row"), P("section", "col", None)),
        check_vma=False,
    )
```

```python
import functools

import jax
import jax.numpy as jnp
from jax import lax
from jax.experimental import pallas as pl
from jax.experimental.pallas import tpu as pltpu
from jax.sharding import PartitionSpec as P

HEAD_DIM = 128
EPSILON = 1e-05
FLOOR = -1e30
MESH = pl.DeviceIdType.MESH
F32 = jnp.float32
BF16 = jnp.bfloat16


def kernel(
    dims,
    hidden_ref,
    gain_hbm,
    qw_ref,
    kvw_ref,
    cache_ref,
    len_hbm,
    handed_ref,
    newkv_ref,
    weights,
    cache,
    keys,
    values,
    gain_ref,
    len_ref,
    scaled_rows,
    gathered,
    parts,
    arrived,
    summed,
    full,
    outs,
    outs_in,
    stat_rows,
    stat_in,
    squares,
    final,
    weight_sem,
    cache_sem,
    small_sem,
    gather_send,
    gather_recv,
    own_send,
    sum_send,
    sum_recv,
    turn_send,
    turn_recv,
    full_send,
    full_recv,
    out_send,
    out_recv,
    stat_send,
    stat_recv,
    square_send,
    square_recv,
    hand_send,
    hand_recv,
):
    n_sec, n_row, n_col, units, quarter, heads_per, pairs_per, kv_heads = dims
    sec, row, col = lax.axis_index("section"), lax.axis_index("row"), lax.axis_index("col")
    rows, width = hidden_ref.shape
    prompts, positions = cache_ref.shape[0], cache_ref.shape[1]
    samples = rows // prompts
    group = (heads_per * n_col) // kv_heads
    tall = group * samples
    mine = kv_heads // n_row
    tile = quarter * HEAD_DIM
    half = width // 2
    is_end = jnp.logical_or(col == 0, col == n_col - 1)

    mate = row + 1 - 2 * (row % 2)
    across = (row + 2) % 4
    far_peer = (mate + 2) % 4

    def peer(d):
        return lax.rem(row + d, n_row)

    own_loads = [
        pltpu.make_async_copy(
            hidden_ref.at[:, pl.ds(h * half, half)], gathered.at[col, h], small_sem.at[h]
        )
        for h in range(2)
    ]
    gain_load = pltpu.make_async_copy(gain_hbm, gain_ref, small_sem.at[2])
    len_load = pltpu.make_async_copy(len_hbm, len_ref, small_sem.at[3])
    cache_load = pltpu.make_async_copy(cache_ref, cache, cache_sem)
    for load in own_loads + [gain_load, len_load, cache_load]:
        load.start()
    loads, filled = [], 0
    for source in (qw_ref, kvw_ref):
        taken = 0
        while taken < source.shape[1]:
            t, at = filled // tile, filled % tile
            wide = min(source.shape[1] - taken, tile - at)
            loads.append(
                pltpu.make_async_copy(
                    source.at[:, pl.ds(taken, wide)],
                    weights.at[t, :, pl.ds(at, wide)],
                    weight_sem.at[len(loads)],
                )
            )
            taken, filled = taken + wide, filled + wide
    barrier = pltpu.get_barrier_semaphore()
    for d in range(1, n_row):
        pl.semaphore_signal(barrier, inc=1, device_id=(sec, peer(d), col), device_id_type=MESH)
    for d in range(1, n_col):
        pl.semaphore_signal(
            barrier, inc=1, device_id=(sec, row, lax.rem(col + d, n_col)), device_id_type=MESH
        )
    pl.semaphore_signal(
        barrier, inc=1, device_id=(lax.rem(sec + n_sec - 1, n_sec), row, col), device_id_type=MESH
    )

    while filled < n_row * tile:
        t, at = filled // tile, filled % tile
        weights[t, :, at:] = jnp.zeros((width, tile - at), BF16)
        filled = (t + 1) * tile
    pl.semaphore_wait(barrier, n_row - 1 + n_col - 1 + 1)

    def gather_copy(block, h, to, send_sem):
        return pltpu.make_async_remote_copy(
            src_ref=gathered.at[block, h],
            dst_ref=gathered.at[block, h],
            send_sem=send_sem.at[h],
            recv_sem=gather_recv.at[block, h],
            device_id=(sec, row, to),
            device_id_type=MESH,
        )

    def own_copy(h, to, send_sem):
        return pltpu.make_async_remote_copy(
            src_ref=hidden_ref.at[:, pl.ds(h * half, half)],
            dst_ref=gathered.at[col, h],
            send_sem=send_sem.at[h],
            recv_sem=gather_recv.at[col, h],
            device_id=(sec, row, to),
            device_id_type=MESH,
        )

    below, above = jnp.maximum(col - 1, 0), jnp.minimum(col + 1, n_col - 1)

    for h in range(2):

        @pl.when(col > 0)
        def _():
            own_copy(h, below, gather_send.at[col]).start()

        @pl.when(col < n_col - 1)
        def _():
            own_copy(h, above, own_send).start()

    for load in loads:
        load.start()

    for load in own_loads:
        load.wait()
    square = jnp.zeros((rows, 1), F32)
    for h in range(2):
        widened = gathered[col, h].astype(F32)
        square = square + jnp.sum(widened * widened, axis=1, keepdims=True)
    squares[row] = jnp.broadcast_to(square, (rows, HEAD_DIM))

    def square_copy(d):
        return pltpu.make_async_remote_copy(
            src_ref=squares.at[row],
            dst_ref=squares.at[row],
            send_sem=square_send.at[d],
            recv_sem=square_recv.at[row],
            device_id=(sec, peer(d), col),
            device_id_type=MESH,
        )

    for d in range(1, n_row):
        square_copy(d).start()

    slots = 2 * positions
    picked = lax.broadcasted_iota(jnp.int32, (slots, slots), 0)
    offered = lax.broadcasted_iota(jnp.int32, (slots, slots), 1)
    wanted = jnp.where(picked < positions, 2 * picked, 2 * (picked - positions) + 1)
    pick = jnp.where(offered == wanted, 1.0, 0.0).astype(BF16)
    cache_load.wait()
    strip = 2 * HEAD_DIM
    strips = cache_ref.shape[3] // strip

    def split(k, carry):
        p = k // strips
        some = pl.ds(pl.multiple_of((k % strips) * strip, strip), strip)
        both = cache[p, :, :, some].reshape(slots, strip)
        apart = jnp.dot(pick, both, preferred_element_type=F32).astype(BF16)
        keys[p, :, some] = apart[:positions]
        values[p, :, some] = apart[positions:]
        return carry

    shorter = jnp.minimum(col, n_col - 1 - col)
    upward = col < n_col - 1 - col

    def block_at(k):
        away = (k + 1) // 2
        near = jnp.where(k % 2 == 1, col + away, col - away)
        far = jnp.where(upward, col + (k - shorter), col - (k - shorter))
        return jnp.where(k <= 2 * shorter, near, far)

    def pass_on(k, h):
        block = block_at(k)
        gather_copy(block, h, below, gather_send.at[block]).wait_recv()

        @pl.when(block > col)
        def _():
            gather_copy(block, h, below, gather_send.at[block]).start()

        @pl.when(block < col)
        def _():
            gather_copy(block, h, above, gather_send.at[block]).start()

    in_middle = jnp.logical_not(is_end)
    ways = prompts * strips
    for h in range(2):
        lax.fori_loop(h * ways // 2, (h + 1) * ways // 2, split, 0)

        @pl.when(in_middle)
        def _():
            for k in range(1, min(3, n_col)):
                pass_on(k, h)

    def pass_late(h):
        @pl.when(in_middle)
        def _():
            for k in range(3, n_col):
                pass_on(k, h)

    def sum_copy(block, other):
        return pltpu.make_async_remote_copy(
            src_ref=parts.at[block, pl.ds(other * quarter, quarter)],
            dst_ref=arrived.at[block, row],
            send_sem=sum_send.at[block, other],
            recv_sem=sum_recv.at[block, row],
            device_id=(sec, other, col),
            device_id_type=MESH,
        )

    def sum_wait(block, d):
        other = peer(d)
        pltpu.make_async_remote_copy(
            src_ref=arrived.at[block, other],
            dst_ref=arrived.at[block, other],
            send_sem=sum_send.at[block, d],
            recv_sem=sum_recv.at[block, other],
            device_id=(sec, other, col),
            device_id_type=MESH,
        ).wait_recv()

    def full_part(source, part):
        return full.at[pl.ds(source * units + part * quarter, quarter)]

    def full_copy(source, part, to, sem):
        return pltpu.make_async_remote_copy(
            src_ref=full_part(source, part),
            dst_ref=full_part(source, part),
            send_sem=full_send.at[source, sem],
            recv_sem=full_recv.at[source, part],
            device_id=(sec, to, col),
            device_id_type=MESH,
        )

    def spread(source):
        full_copy(source, row, across, 0).start()
        full_copy(source, row, mate, 1).start()

    def relay(source):
        full_copy(source, across, mate, 2).wait_recv()
        full_copy(source, across, mate, 2).start()

    def turn_copy(block):
        return pltpu.make_async_remote_copy(
            src_ref=summed.at[block],
            dst_ref=full_part(col, row),
            send_sem=turn_send.at[block],
            recv_sem=turn_recv.at[col],
            device_id=(sec, row, block),
            device_id_type=MESH,
        )

    def reduce_block(block):
        total = parts[block, pl.ds(row * quarter, quarter)].astype(F32)
        for d in range(1, n_row):
            sum_wait(block, d)
            total = total + arrived[block, peer(d)].astype(F32)
        total = total.astype(BF16)

        @pl.when(block == col)
        def _():
            full[pl.ds(col * units + row * quarter, quarter)] = total
            spread(col)

        @pl.when(block != col)
        def _():
            summed[block] = total
            turn_copy(block).start()

    for load in loads:
        load.wait()

    gain_load.wait()

    def target(j):
        return jnp.where(
            j == 0, across, jnp.where(j == 1, far_peer, jnp.where(j == 2, mate, row))
        )

    def step(first, count, before, between):
        blocks = [block_at(first + i) for i in range(count)]

        @pl.when(is_end)
        def _():
            for i, block in enumerate(blocks):

                @pl.when(first + i > 0)
                def _():
                    for h in range(2):
                        gather_copy(block, h, below, gather_send.at[block]).wait_recv()

        before()
        for i, block in enumerate(blocks):
            for h in range(2):
                raw = gathered[block, h].astype(F32)
                scaled_rows[h, i * rows : (i + 1) * rows] = (
                    raw * gain_ref[:, h * half : (h + 1) * half]
                ).astype(BF16)

        def multiply(j, carry):
            dest = target(j)
            product = jnp.zeros((count * rows, tile), F32)
            for h in range(2):
                product = product + jnp.dot(
                    scaled_rows[h, : count * rows],
                    weights[dest, h * half : (h + 1) * half],
                    preferred_element_type=F32,
                )
            product = product.astype(BF16)
            for i, block in enumerate(blocks):
                for u in range(quarter):
                    parts[block, dest * quarter + u] = product[
                        i * rows : (i + 1) * rows, u * HEAD_DIM : (u + 1) * HEAD_DIM
                    ]

            @pl.when(j < n_row - 1)
            def _():
                for block in blocks:
                    sum_copy(block, dest).start()

            return carry

        lax.fori_loop(0, n_row // 2, multiply, 0)
        between()
        lax.fori_loop(n_row // 2, n_row, multiply, 0)

    step(0, 2, lambda: pass_late(0), lambda: pass_late(1))

    def single(k, carry):
        def between():
            @pl.when(k == 2)
            def _():
                reduce_block(block_at(0))

            reduce_block(block_at(k - 1))

        step(k, 1, lambda: None, between)
        return carry

    lax.fori_loop(2, n_col, single, 0)
    reduce_block(block_at(n_col - 1))

    relay(col)

    for d in range(1, n_row):
        other = peer(d)
        pltpu.make_async_remote_copy(
            src_ref=squares.at[other],
            dst_ref=squares.at[other],
            send_sem=square_send.at[d],
            recv_sem=square_recv.at[other],
            device_id=(sec, other, col),
            device_id_type=MESH,
        ).wait_recv()
    square_sum = squares[0]
    for i in range(1, n_row):
        square_sum = square_sum + squares[i]
    len_load.wait()
    scaling = lax.rsqrt(square_sum / (width * n_row) + EPSILON)

    def head_unit(head):
        return (head // heads_per) * units + head % heads_per

    def pair_unit(pair):
        return (pair // pairs_per) * units + heads_per + pair % pairs_per

    def scaled(unit, p):
        some = pl.ds(p * samples, samples)
        factor = scaling[p * samples : (p + 1) * samples]
        return (full[unit, some, :].astype(F32) * factor).astype(BF16)

    def queries(g, p):
        return jnp.concatenate([scaled(head_unit(g * group + i), p) for i in range(group)], axis=0)

    score_scale = HEAD_DIM ** (-0.5)
    lane = lax.broadcasted_iota(jnp.int32, (tall, HEAD_DIM), 1)
    position = row * positions + lax.broadcasted_iota(jnp.int32, (1, positions), 1)
    valid = [position < len_ref[0, p] for p in range(prompts)]

    def attend(heads):
        pairs = [(g, p) for g in heads for p in range(prompts)]

        def some(g):
            return pl.ds(pl.multiple_of(g * HEAD_DIM, HEAD_DIM), HEAD_DIM)

        scores = [
            lax.dot_general(
                queries(g, p),
                keys[p, :, some(g)],
                (((1,), (1,)), ((), ())),
                preferred_element_type=F32,
            )
            for g, p in pairs
        ]
        scores = [
            jnp.where(valid[p], score * score_scale, FLOOR)
            for (g, p), score in zip(pairs, scores)
        ]
        tops = [jnp.max(score, axis=1, keepdims=True) for score in scores]
        raised = [
            jnp.where(valid[p], jnp.exp(score - top), 0.0)
            for (g, p), score, top in zip(pairs, scores, tops)
        ]
        totals = [jnp.sum(weight, axis=1, keepdims=True) for weight in raised]
        products = [
            jnp.dot(weight.astype(BF16), values[p, :, some(g)], preferred_element_type=F32)
            for (g, p), weight in zip(pairs, raised)
        ]
        for (g, p), product in zip(pairs, products):
            outs[g, p] = product.astype(BF16)
        for i, g in enumerate(heads):
            both = jnp.zeros((tall, HEAD_DIM), F32)
            for p in range(prompts):
                both = jnp.where(lane == 2 * p, tops[i * prompts + p], both)
                both = jnp.where(lane == 2 * p + 1, totals[i * prompts + p], both)
            stat_rows[g] = both.T[:8]

    def out_copy(dest):
        return pltpu.make_async_remote_copy(
            src_ref=outs.at[pl.ds(dest * mine, mine)],
            dst_ref=outs_in.at[row],
            send_sem=out_send.at[dest],
            recv_sem=out_recv.at[row],
            device_id=(sec, dest, col),
            device_id_type=MESH,
        )

    chunk_heads = max(1, heads_per // group)
    chunk_cols = max(1, group // heads_per)
    chunks = kv_heads // chunk_heads
    by_dest = chunks == n_row and chunk_heads == mine and chunks == n_col
    col_turn = jnp.where(
        col == across, 0, jnp.where(col == far_peer, 1, jnp.where(col == mate, 2, 3))
    )

    def stat_copy(dest):
        return pltpu.make_async_remote_copy(
            src_ref=stat_rows.at[pl.ds(dest * mine, mine)],
            dst_ref=stat_in.at[row],
            send_sem=stat_send.at[dest],
            recv_sem=stat_recv.at[row],
            device_id=(sec, dest, col),
            device_id_type=MESH,
        )

    def chunk(k, carry):
        j = k
        if by_dest:
            j = jnp.where(k == 0, col, target(jnp.where(k > col_turn, k, k - 1)))
        for i in range(chunk_cols):
            source = j * chunk_cols + i
            full_copy(source, mate, mate, 1).wait_recv()
            full_copy(source, far_peer, mate, 2).wait_recv()
        attend([j * chunk_heads + i for i in range(chunk_heads)])
        last = j * chunk_heads + chunk_heads - 1
        dest = last // mine

        @pl.when(jnp.logical_and(last % mine == mine - 1, dest != row))
        def _():
            out_copy(dest).start()
            stat_copy(dest).start()

        return carry

    early = 1 if by_dest else 0
    lax.fori_loop(0, early, chunk, 0)

    def forward(k, carry):
        source = block_at(k)
        pltpu.make_async_remote_copy(
            src_ref=full_part(source, row),
            dst_ref=full_part(source, row),
            send_sem=turn_send.at[source],
            recv_sem=turn_recv.at[source],
            device_id=(sec, row, source),
            device_id_type=MESH,
        ).wait_recv()
        spread(source)

        @pl.when(k > 1)
        def _():
            relay(block_at(k - 1))

        return carry

    lax.fori_loop(1, n_col, forward, 0)

    @pl.when(n_col > 1)
    def _():
        relay(block_at(n_col - 1))
    lax.fori_loop(early, chunks, chunk, 0)

    outs_in[row] = outs[pl.ds(row * mine, mine)]
    stat_in[row] = stat_rows[pl.ds(row * mine, mine)]

    for pair in range(2 * kv_heads):
        newkv_ref[:, pair * HEAD_DIM : (pair + 1) * HEAD_DIM] = (
            full[pair_unit(pair)].astype(F32) * scaling
        ).astype(BF16)

    def own_part(g, p):
        new_key = jnp.concatenate([scaled(pair_unit(g), p)] * group, axis=0)
        product = queries(g, p).astype(F32) * new_key.astype(F32)
        return jnp.sum(product, axis=1, keepdims=True) * score_scale

    own_scores = [[own_part(row * mine + i, p) for p in range(prompts)] for i in range(mine)]

    for d in range(1, n_row):
        other = peer(d)
        pltpu.make_async_remote_copy(
            src_ref=stat_in.at[other],
            dst_ref=stat_in.at[other],
            send_sem=stat_send.at[other],
            recv_sem=stat_recv.at[other],
            device_id=(sec, other, col),
            device_id_type=MESH,
        ).wait_recv()
        pltpu.make_async_remote_copy(
            src_ref=outs_in.at[other],
            dst_ref=outs_in.at[other],
            send_sem=out_send.at[other],
            recv_sem=out_recv.at[other],
            device_id=(sec, other, col),
            device_id_type=MESH,
        ).wait_recv()

    lines = stat_in[...].reshape(n_row * mine * 8, tall)
    stats = jnp.concatenate([lines, jnp.zeros((HEAD_DIM - n_row * mine * 8, tall), F32)], axis=0).T
    span = group * HEAD_DIM

    def hand_copy(i, p):
        piece = (pl.ds(p * samples, samples), pl.ds(i * span, span))
        return pltpu.make_async_remote_copy(
            src_ref=final.at[piece],
            dst_ref=handed_ref.at[piece],
            send_sem=hand_send.at[i, p],
            recv_sem=hand_recv.at[i, p],
            device_id=(lax.rem(sec + 1, n_sec), row, col),
            device_id_type=MESH,
        )

    for i in range(mine):
        g = row * mine + i
        for p in range(prompts):
            new_value = jnp.concatenate([scaled(pair_unit(kv_heads + g), p)] * group, axis=0)
            own = own_scores[i][p]
            top = own
            tops, totals = [], []
            for s in range(n_row):
                at = (s * mine + i) * 8 + 2 * p
                tops.append(stats[:, at : at + 1])
                totals.append(stats[:, at + 1 : at + 2])
                top = jnp.maximum(top, tops[-1])
            own_weight = jnp.exp(own - top)
            total = own_weight
            value = own_weight.astype(BF16).astype(F32) * new_value.astype(F32)
            for s in range(n_row):
                keep = jnp.exp(tops[s] - top)
                total = total + keep * totals[s]
                value = value + keep * outs_in[s, i, p].astype(F32)
            done = (value / total).astype(BF16)
            for h in range(group):
                first = (i * group + h) * HEAD_DIM
                final[p * samples : (p + 1) * samples, first : first + HEAD_DIM] = done[
                    h * samples : (h + 1) * samples
                ]
            hand_copy(i, p).start()

    for h in range(2):

        @pl.when(col > 0)
        def _():
            own_copy(h, below, gather_send.at[col]).wait_send()

        @pl.when(col < n_col - 1)
        def _():
            own_copy(h, above, own_send).wait_send()

    def drain(k, carry):
        block = block_at(k)

        @pl.when(jnp.logical_and(block != col, jnp.logical_not(is_end)))
        def _():
            for h in range(2):
                gather_copy(block, h, below, gather_send.at[block]).wait_send()

        @pl.when(block != col)
        def _():
            turn_copy(block).wait_send()

        for d in range(1, n_row):
            sum_copy(block, peer(d)).wait_send()
        full_copy(block, row, across, 0).wait_send()
        full_copy(block, row, mate, 1).wait_send()
        full_copy(block, across, mate, 2).wait_send()
        return carry

    lax.fori_loop(0, n_col, drain, 0)
    for d in range(1, n_row):
        square_copy(d).wait_send()
        stat_copy(peer(d)).wait_send()
        out_copy(peer(d)).wait_send()
    for i in range(mine):
        for p in range(prompts):
            hand_copy(i, p).wait()


def shards(n_sec, n_row, n_col, hidden_in, norm_gain, q_weight, kv_weight, kv_cache, lengths):
    _, rows, width = hidden_in.shape
    _, prompts, positions, _, cache_width = kv_cache.shape
    kv_heads = cache_width // HEAD_DIM
    heads_per = q_weight.shape[2] // HEAD_DIM
    pairs_per = kv_weight.shape[2] // HEAD_DIM
    units = -(-(heads_per + pairs_per) // 4) * 4
    quarter = units // n_row
    group = heads_per * n_col // kv_heads
    tall = group * (rows // prompts)
    mine = kv_heads // n_row
    dims = (n_sec, n_row, n_col, units, quarter, heads_per, pairs_per, kv_heads)
    dma = pltpu.SemaphoreType.DMA
    handed, new_kv = pl.pallas_call(
        functools.partial(kernel, dims),
        out_shape=(
            jax.ShapeDtypeStruct((rows, heads_per * n_col // n_row * HEAD_DIM), BF16),
            jax.ShapeDtypeStruct((rows, 2 * cache_width), BF16),
        ),
        in_specs=[pl.BlockSpec(memory_space=pltpu.HBM)] * 6,
        out_specs=[pl.BlockSpec(memory_space=pltpu.VMEM)] * 2,
        scratch_shapes=[
            pltpu.VMEM((n_row, width, quarter * HEAD_DIM), BF16),
            pltpu.VMEM((prompts, positions, 2, cache_width), BF16),
            pltpu.VMEM((prompts, positions, cache_width), BF16),
            pltpu.VMEM((prompts, positions, cache_width), BF16),
            pltpu.VMEM((1, width), F32),
            pltpu.SMEM((1, prompts), jnp.int32),
            pltpu.VMEM((2, 2 * rows, width // 2), BF16),
            pltpu.VMEM((n_col, 2, rows, width // 2), BF16),
            pltpu.VMEM((n_col, units, rows, HEAD_DIM), BF16),
            pltpu.VMEM((n_col, n_row, quarter, rows, HEAD_DIM), BF16),
            pltpu.VMEM((n_col, quarter, rows, HEAD_DIM), BF16),
            pltpu.VMEM((n_col * units, rows, HEAD_DIM), BF16),
            pltpu.VMEM((kv_heads, prompts, tall, HEAD_DIM), BF16),
            pltpu.VMEM((n_row, mine, prompts, tall, HEAD_DIM), BF16),
            pltpu.VMEM((kv_heads, 8, tall), F32),
            pltpu.VMEM((n_row, mine, 8, tall), F32),
            pltpu.VMEM((n_row, rows, HEAD_DIM), F32),
            pltpu.VMEM((rows, heads_per * n_col // n_row * HEAD_DIM), BF16),
            dma((2 * n_row + 2,)),
            dma,
            dma((4,)),
            dma((n_col, 2)),
            dma((n_col, 2)),
            dma((2,)),
            dma((n_col, n_row)),
            dma((n_col, n_row)),
            dma((n_col,)),
            dma((n_col,)),
            dma((n_col, n_row)),
            dma((n_col, n_row)),
            dma((n_row,)),
            dma((n_row,)),
            dma((n_row,)),
            dma((n_row,)),
            dma((n_row,)),
            dma((n_row,)),
            dma((mine, prompts)),
            dma((mine, prompts)),
        ],
        compiler_params=pltpu.CompilerParams(
            collective_id=0, has_side_effects=True, vmem_limit_bytes=54912 * 1024
        ),
    )(
        hidden_in[0],
        norm_gain,
        q_weight[0],
        kv_weight[0],
        kv_cache[0],
        lengths,
    )
    return handed[None], new_kv[None]


def solution(mesh):
    n_sec, n_row, n_col = (mesh.shape[name] for name in ("section", "row", "col"))
    return jax.shard_map(
        functools.partial(shards, n_sec, n_row, n_col),
        mesh=mesh,
        in_specs=(
            P("section", "col", "row"),
            P("section", "row"),
            P("section", "row", "col"),
            P("section", "row", "col"),
            P("section", "col", "row", None, None),
            P("section", "col"),
        ),
        out_specs=(P("section", "col", "row"), P("section", "col", None)),
        check_vma=False,
    )
```

```python
import functools

import jax
import jax.numpy as jnp
from jax import lax
from jax.experimental import pallas as pl
from jax.experimental.pallas import tpu as pltpu
from jax.sharding import PartitionSpec as P

HEAD_DIM = 128
EPSILON = 1e-05
FLOOR = -1e30
MESH = pl.DeviceIdType.MESH
F32 = jnp.float32
BF16 = jnp.bfloat16


def kernel(
    dims,
    hidden_ref,
    gain_hbm,
    qw_ref,
    kvw_ref,
    cache_ref,
    len_hbm,
    handed_ref,
    newkv_ref,
    weights,
    cache,
    keys,
    values,
    gain_ref,
    len_ref,
    scaled_rows,
    gathered,
    parts,
    arrived,
    summed,
    full,
    outs,
    outs_in,
    stat_rows,
    stat_in,
    squares,
    final,
    weight_sem,
    cache_sem,
    small_sem,
    gather_send,
    gather_recv,
    own_send,
    sum_send,
    sum_recv,
    turn_send,
    turn_recv,
    full_send,
    full_recv,
    out_send,
    out_recv,
    stat_send,
    stat_recv,
    square_send,
    square_recv,
    hand_send,
    hand_recv,
):
    n_sec, n_row, n_col, units, quarter, heads_per, pairs_per, kv_heads = dims
    sec, row, col = lax.axis_index("section"), lax.axis_index("row"), lax.axis_index("col")
    rows, width = hidden_ref.shape
    prompts, positions = cache_ref.shape[0], cache_ref.shape[1]
    samples = rows // prompts
    group = (heads_per * n_col) // kv_heads
    tall = group * samples
    mine = kv_heads // n_row
    tile = quarter * HEAD_DIM
    half = width // 2
    is_end = jnp.logical_or(col == 0, col == n_col - 1)

    mate = row + 1 - 2 * (row % 2)
    across = (row + 2) % 4
    far_peer = (mate + 2) % 4

    def peer(d):
        return lax.rem(row + d, n_row)

    own_loads = [
        pltpu.make_async_copy(
            hidden_ref.at[:, pl.ds(h * half, half)], gathered.at[col, h], small_sem.at[h]
        )
        for h in range(2)
    ]
    gain_load = pltpu.make_async_copy(gain_hbm, gain_ref, small_sem.at[2])
    len_load = pltpu.make_async_copy(len_hbm, len_ref, small_sem.at[3])
    cache_load = pltpu.make_async_copy(cache_ref, cache, cache_sem)
    for load in own_loads + [gain_load, len_load, cache_load]:
        load.start()
    loads, filled = [], 0
    for source in (qw_ref, kvw_ref):
        taken = 0
        while taken < source.shape[1]:
            t, at = filled // tile, filled % tile
            wide = min(source.shape[1] - taken, tile - at)
            loads.append(
                pltpu.make_async_copy(
                    source.at[:, pl.ds(taken, wide)],
                    weights.at[t, :, pl.ds(at, wide)],
                    weight_sem.at[len(loads)],
                )
            )
            taken, filled = taken + wide, filled + wide
    barrier = pltpu.get_barrier_semaphore()
    for d in range(1, n_row):
        pl.semaphore_signal(barrier, inc=1, device_id=(sec, peer(d), col), device_id_type=MESH)
    for d in range(1, n_col):
        pl.semaphore_signal(
            barrier, inc=1, device_id=(sec, row, lax.rem(col + d, n_col)), device_id_type=MESH
        )
    pl.semaphore_signal(
        barrier, inc=1, device_id=(lax.rem(sec + n_sec - 1, n_sec), row, col), device_id_type=MESH
    )

    while filled < n_row * tile:
        t, at = filled // tile, filled % tile
        weights[t, :, at:] = jnp.zeros((width, tile - at), BF16)
        filled = (t + 1) * tile
    pl.semaphore_wait(barrier, n_row - 1 + n_col - 1 + 1)

    def gather_copy(block, h, to, send_sem):
        return pltpu.make_async_remote_copy(
            src_ref=gathered.at[block, h],
            dst_ref=gathered.at[block, h],
            send_sem=send_sem.at[h],
            recv_sem=gather_recv.at[block, h],
            device_id=(sec, row, to),
            device_id_type=MESH,
        )

    def own_copy(h, to, send_sem):
        return pltpu.make_async_remote_copy(
            src_ref=hidden_ref.at[:, pl.ds(h * half, half)],
            dst_ref=gathered.at[col, h],
            send_sem=send_sem.at[h],
            recv_sem=gather_recv.at[col, h],
            device_id=(sec, row, to),
            device_id_type=MESH,
        )

    below, above = jnp.maximum(col - 1, 0), jnp.minimum(col + 1, n_col - 1)

    for h in range(2):

        @pl.when(col > 0)
        def _():
            own_copy(h, below, gather_send.at[col]).start()

        @pl.when(col < n_col - 1)
        def _():
            own_copy(h, above, own_send).start()

    for load in loads:
        load.start()

    for load in own_loads:
        load.wait()
    square = jnp.zeros((rows, 1), F32)
    for h in range(2):
        widened = gathered[col, h].astype(F32)
        square = square + jnp.sum(widened * widened, axis=1, keepdims=True)
    squares[row] = jnp.broadcast_to(square, (rows, HEAD_DIM))

    def square_copy(d):
        return pltpu.make_async_remote_copy(
            src_ref=squares.at[row],
            dst_ref=squares.at[row],
            send_sem=square_send.at[d],
            recv_sem=square_recv.at[row],
            device_id=(sec, peer(d), col),
            device_id_type=MESH,
        )

    for d in range(1, n_row):
        square_copy(d).start()

    slots = 2 * positions
    picked = lax.broadcasted_iota(jnp.int32, (slots, slots), 0)
    offered = lax.broadcasted_iota(jnp.int32, (slots, slots), 1)
    wanted = jnp.where(picked < positions, 2 * picked, 2 * (picked - positions) + 1)
    pick = jnp.where(offered == wanted, 1.0, 0.0).astype(BF16)
    cache_load.wait()
    strip = 2 * HEAD_DIM
    strips = cache_ref.shape[3] // strip

    def split(k, carry):
        p = k // strips
        some = pl.ds(pl.multiple_of((k % strips) * strip, strip), strip)
        both = cache[p, :, :, some].reshape(slots, strip)
        apart = jnp.dot(pick, both, preferred_element_type=F32).astype(BF16)
        keys[p, :, some] = apart[:positions]
        values[p, :, some] = apart[positions:]
        return carry

    shorter = jnp.minimum(col, n_col - 1 - col)
    upward = col < n_col - 1 - col

    def block_at(k):
        away = (k + 1) // 2
        near = jnp.where(k % 2 == 1, col + away, col - away)
        far = jnp.where(upward, col + (k - shorter), col - (k - shorter))
        return jnp.where(k <= 2 * shorter, near, far)

    def pass_on(k, h):
        block = block_at(k)
        gather_copy(block, h, below, gather_send.at[block]).wait_recv()

        @pl.when(block > col)
        def _():
            gather_copy(block, h, below, gather_send.at[block]).start()

        @pl.when(block < col)
        def _():
            gather_copy(block, h, above, gather_send.at[block]).start()

    in_middle = jnp.logical_not(is_end)
    ways = prompts * strips
    for h in range(2):
        lax.fori_loop(h * ways // 2, (h + 1) * ways // 2, split, 0)

        @pl.when(in_middle)
        def _():
            for k in range(1, min(3, n_col)):
                pass_on(k, h)

    def pass_late(h):
        @pl.when(in_middle)
        def _():
            for k in range(3, n_col):
                pass_on(k, h)

    def sum_copy(block, other):
        return pltpu.make_async_remote_copy(
            src_ref=parts.at[block, pl.ds(other * quarter, quarter)],
            dst_ref=arrived.at[block, row],
            send_sem=sum_send.at[block, other],
            recv_sem=sum_recv.at[block, row],
            device_id=(sec, other, col),
            device_id_type=MESH,
        )

    def sum_wait(block, d):
        other = peer(d)
        pltpu.make_async_remote_copy(
            src_ref=arrived.at[block, other],
            dst_ref=arrived.at[block, other],
            send_sem=sum_send.at[block, d],
            recv_sem=sum_recv.at[block, other],
            device_id=(sec, other, col),
            device_id_type=MESH,
        ).wait_recv()

    def full_part(source, part):
        return full.at[pl.ds(source * units + part * quarter, quarter)]

    def full_copy(source, part, to, sem):
        return pltpu.make_async_remote_copy(
            src_ref=full_part(source, part),
            dst_ref=full_part(source, part),
            send_sem=full_send.at[source, sem],
            recv_sem=full_recv.at[source, part],
            device_id=(sec, to, col),
            device_id_type=MESH,
        )

    def spread(source):
        full_copy(source, row, across, 0).start()
        full_copy(source, row, far_peer, 2).start()
        full_copy(source, row, mate, 1).start()

    def relay(source):
        full_copy(source, across, mate, 2).wait_recv()

    def turn_copy(block):
        return pltpu.make_async_remote_copy(
            src_ref=summed.at[block],
            dst_ref=full_part(col, row),
            send_sem=turn_send.at[block],
            recv_sem=turn_recv.at[col],
            device_id=(sec, row, block),
            device_id_type=MESH,
        )

    def reduce_block(block):
        total = parts[block, pl.ds(row * quarter, quarter)].astype(F32)
        for d in range(1, n_row):
            sum_wait(block, d)
            total = total + arrived[block, peer(d)].astype(F32)
        total = total.astype(BF16)

        @pl.when(block == col)
        def _():
            full[pl.ds(col * units + row * quarter, quarter)] = total
            spread(col)

        @pl.when(block != col)
        def _():
            summed[block] = total
            turn_copy(block).start()

    for load in loads:
        load.wait()

    gain_load.wait()

    def target(j):
        return jnp.where(
            j == 0, across, jnp.where(j == 1, far_peer, jnp.where(j == 2, mate, row))
        )

    def step(first, count, before, between):
        blocks = [block_at(first + i) for i in range(count)]

        @pl.when(is_end)
        def _():
            for i, block in enumerate(blocks):

                @pl.when(first + i > 0)
                def _():
                    for h in range(2):
                        gather_copy(block, h, below, gather_send.at[block]).wait_recv()

        before()
        for i, block in enumerate(blocks):
            for h in range(2):
                raw = gathered[block, h].astype(F32)
                scaled_rows[h, i * rows : (i + 1) * rows] = (
                    raw * gain_ref[:, h * half : (h + 1) * half]
                ).astype(BF16)

        def multiply(j, carry):
            dest = target(j)
            product = jnp.zeros((count * rows, tile), F32)
            for h in range(2):
                product = product + jnp.dot(
                    scaled_rows[h, : count * rows],
                    weights[dest, h * half : (h + 1) * half],
                    preferred_element_type=F32,
                )
            product = product.astype(BF16)
            for i, block in enumerate(blocks):
                for u in range(quarter):
                    parts[block, dest * quarter + u] = product[
                        i * rows : (i + 1) * rows, u * HEAD_DIM : (u + 1) * HEAD_DIM
                    ]

            @pl.when(j < n_row - 1)
            def _():
                for block in blocks:
                    sum_copy(block, dest).start()

            return carry

        lax.fori_loop(0, n_row // 2, multiply, 0)
        between()
        lax.fori_loop(n_row // 2, n_row, multiply, 0)

    step(0, 2, lambda: pass_late(0), lambda: pass_late(1))

    def single(k, carry):
        def between():
            @pl.when(k == 2)
            def _():
                reduce_block(block_at(0))

            reduce_block(block_at(k - 1))

        step(k, 1, lambda: None, between)
        return carry

    lax.fori_loop(2, n_col, single, 0)
    reduce_block(block_at(n_col - 1))

    relay(col)

    for d in range(1, n_row):
        other = peer(d)
        pltpu.make_async_remote_copy(
            src_ref=squares.at[other],
            dst_ref=squares.at[other],
            send_sem=square_send.at[d],
            recv_sem=square_recv.at[other],
            device_id=(sec, other, col),
            device_id_type=MESH,
        ).wait_recv()
    square_sum = squares[0]
    for i in range(1, n_row):
        square_sum = square_sum + squares[i]
    len_load.wait()
    scaling = lax.rsqrt(square_sum / (width * n_row) + EPSILON)

    def head_unit(head):
        return (head // heads_per) * units + head % heads_per

    def pair_unit(pair):
        return (pair // pairs_per) * units + heads_per + pair % pairs_per

    def scaled(unit, p):
        some = pl.ds(p * samples, samples)
        factor = scaling[p * samples : (p + 1) * samples]
        return (full[unit, some, :].astype(F32) * factor).astype(BF16)

    def queries(g, p):
        return jnp.concatenate([scaled(head_unit(g * group + i), p) for i in range(group)], axis=0)

    score_scale = HEAD_DIM ** (-0.5)
    lane = lax.broadcasted_iota(jnp.int32, (tall, HEAD_DIM), 1)
    position = row * positions + lax.broadcasted_iota(jnp.int32, (1, positions), 1)
    valid = [position < len_ref[0, p] for p in range(prompts)]

    def attend(heads):
        pairs = [(g, p) for g in heads for p in range(prompts)]

        def some(g):
            return pl.ds(pl.multiple_of(g * HEAD_DIM, HEAD_DIM), HEAD_DIM)

        scores = [
            lax.dot_general(
                queries(g, p),
                keys[p, :, some(g)],
                (((1,), (1,)), ((), ())),
                preferred_element_type=F32,
            )
            for g, p in pairs
        ]
        scores = [
            jnp.where(valid[p], score * score_scale, FLOOR)
            for (g, p), score in zip(pairs, scores)
        ]
        tops = [jnp.max(score, axis=1, keepdims=True) for score in scores]
        raised = [
            jnp.where(valid[p], jnp.exp(score - top), 0.0)
            for (g, p), score, top in zip(pairs, scores, tops)
        ]
        totals = [jnp.sum(weight, axis=1, keepdims=True) for weight in raised]
        products = [
            jnp.dot(weight.astype(BF16), values[p, :, some(g)], preferred_element_type=F32)
            for (g, p), weight in zip(pairs, raised)
        ]
        for (g, p), product in zip(pairs, products):
            outs[g, p] = product.astype(BF16)
        for i, g in enumerate(heads):
            both = jnp.zeros((tall, HEAD_DIM), F32)
            for p in range(prompts):
                both = jnp.where(lane == 2 * p, tops[i * prompts + p], both)
                both = jnp.where(lane == 2 * p + 1, totals[i * prompts + p], both)
            stat_rows[g] = both.T[:8]

    def out_copy(dest):
        return pltpu.make_async_remote_copy(
            src_ref=outs.at[pl.ds(dest * mine, mine)],
            dst_ref=outs_in.at[row],
            send_sem=out_send.at[dest],
            recv_sem=out_recv.at[row],
            device_id=(sec, dest, col),
            device_id_type=MESH,
        )

    chunk_heads = max(1, heads_per // group)
    chunk_cols = max(1, group // heads_per)
    chunks = kv_heads // chunk_heads
    by_dest = chunks == n_row and chunk_heads == mine and chunks == n_col
    col_turn = jnp.where(
        col == across, 0, jnp.where(col == far_peer, 1, jnp.where(col == mate, 2, 3))
    )

    def stat_copy(dest):
        return pltpu.make_async_remote_copy(
            src_ref=stat_rows.at[pl.ds(dest * mine, mine)],
            dst_ref=stat_in.at[row],
            send_sem=stat_send.at[dest],
            recv_sem=stat_recv.at[row],
            device_id=(sec, dest, col),
            device_id_type=MESH,
        )

    def chunk(k, carry):
        j = k
        if by_dest:
            j = jnp.where(k == 0, col, target(jnp.where(k > col_turn, k, k - 1)))
        for i in range(chunk_cols):
            source = j * chunk_cols + i
            full_copy(source, mate, mate, 1).wait_recv()
            full_copy(source, far_peer, mate, 2).wait_recv()
        attend([j * chunk_heads + i for i in range(chunk_heads)])
        last = j * chunk_heads + chunk_heads - 1
        dest = last // mine

        @pl.when(jnp.logical_and(last % mine == mine - 1, dest != row))
        def _():
            out_copy(dest).start()
            stat_copy(dest).start()

        return carry

    early = 1 if by_dest else 0
    lax.fori_loop(0, early, chunk, 0)

    def forward(k, carry):
        source = block_at(k)
        pltpu.make_async_remote_copy(
            src_ref=full_part(source, row),
            dst_ref=full_part(source, row),
            send_sem=turn_send.at[source],
            recv_sem=turn_recv.at[source],
            device_id=(sec, row, source),
            device_id_type=MESH,
        ).wait_recv()
        spread(source)

        @pl.when(k > 1)
        def _():
            relay(block_at(k - 1))

        return carry

    lax.fori_loop(1, n_col, forward, 0)

    @pl.when(n_col > 1)
    def _():
        relay(block_at(n_col - 1))
    lax.fori_loop(early, chunks, chunk, 0)

    outs_in[row] = outs[pl.ds(row * mine, mine)]
    stat_in[row] = stat_rows[pl.ds(row * mine, mine)]

    for pair in range(2 * kv_heads):
        newkv_ref[:, pair * HEAD_DIM : (pair + 1) * HEAD_DIM] = (
            full[pair_unit(pair)].astype(F32) * scaling
        ).astype(BF16)

    def own_part(g, p):
        new_key = jnp.concatenate([scaled(pair_unit(g), p)] * group, axis=0)
        product = queries(g, p).astype(F32) * new_key.astype(F32)
        return jnp.sum(product, axis=1, keepdims=True) * score_scale

    own_scores = [[own_part(row * mine + i, p) for p in range(prompts)] for i in range(mine)]

    for d in range(1, n_row):
        other = peer(d)
        pltpu.make_async_remote_copy(
            src_ref=stat_in.at[other],
            dst_ref=stat_in.at[other],
            send_sem=stat_send.at[other],
            recv_sem=stat_recv.at[other],
            device_id=(sec, other, col),
            device_id_type=MESH,
        ).wait_recv()
        pltpu.make_async_remote_copy(
            src_ref=outs_in.at[other],
            dst_ref=outs_in.at[other],
            send_sem=out_send.at[other],
            recv_sem=out_recv.at[other],
            device_id=(sec, other, col),
            device_id_type=MESH,
        ).wait_recv()

    lines = stat_in[...].reshape(n_row * mine * 8, tall)
    stats = jnp.concatenate([lines, jnp.zeros((HEAD_DIM - n_row * mine * 8, tall), F32)], axis=0).T
    span = group * HEAD_DIM

    def hand_copy(i, p):
        piece = (pl.ds(p * samples, samples), pl.ds(i * span, span))
        return pltpu.make_async_remote_copy(
            src_ref=final.at[piece],
            dst_ref=handed_ref.at[piece],
            send_sem=hand_send.at[i, p],
            recv_sem=hand_recv.at[i, p],
            device_id=(lax.rem(sec + 1, n_sec), row, col),
            device_id_type=MESH,
        )

    for i in range(mine):
        g = row * mine + i
        for p in range(prompts):
            new_value = jnp.concatenate([scaled(pair_unit(kv_heads + g), p)] * group, axis=0)
            own = own_scores[i][p]
            top = own
            tops, totals = [], []
            for s in range(n_row):
                at = (s * mine + i) * 8 + 2 * p
                tops.append(stats[:, at : at + 1])
                totals.append(stats[:, at + 1 : at + 2])
                top = jnp.maximum(top, tops[-1])
            own_weight = jnp.exp(own - top)
            total = own_weight
            value = own_weight.astype(BF16).astype(F32) * new_value.astype(F32)
            for s in range(n_row):
                keep = jnp.exp(tops[s] - top)
                total = total + keep * totals[s]
                value = value + keep * outs_in[s, i, p].astype(F32)
            done = (value / total).astype(BF16)
            for h in range(group):
                first = (i * group + h) * HEAD_DIM
                final[p * samples : (p + 1) * samples, first : first + HEAD_DIM] = done[
                    h * samples : (h + 1) * samples
                ]
            hand_copy(i, p).start()

    for h in range(2):

        @pl.when(col > 0)
        def _():
            own_copy(h, below, gather_send.at[col]).wait_send()

        @pl.when(col < n_col - 1)
        def _():
            own_copy(h, above, own_send).wait_send()

    def drain(k, carry):
        block = block_at(k)

        @pl.when(jnp.logical_and(block != col, jnp.logical_not(is_end)))
        def _():
            for h in range(2):
                gather_copy(block, h, below, gather_send.at[block]).wait_send()

        @pl.when(block != col)
        def _():
            turn_copy(block).wait_send()

        for d in range(1, n_row):
            sum_copy(block, peer(d)).wait_send()
        full_copy(block, row, across, 0).wait_send()
        full_copy(block, row, mate, 1).wait_send()
        full_copy(block, row, far_peer, 2).wait_send()
        return carry

    lax.fori_loop(0, n_col, drain, 0)
    for d in range(1, n_row):
        square_copy(d).wait_send()
        stat_copy(peer(d)).wait_send()
        out_copy(peer(d)).wait_send()
    for i in range(mine):
        for p in range(prompts):
            hand_copy(i, p).wait()


def shards(n_sec, n_row, n_col, hidden_in, norm_gain, q_weight, kv_weight, kv_cache, lengths):
    _, rows, width = hidden_in.shape
    _, prompts, positions, _, cache_width = kv_cache.shape
    kv_heads = cache_width // HEAD_DIM
    heads_per = q_weight.shape[2] // HEAD_DIM
    pairs_per = kv_weight.shape[2] // HEAD_DIM
    units = -(-(heads_per + pairs_per) // 4) * 4
    quarter = units // n_row
    group = heads_per * n_col // kv_heads
    tall = group * (rows // prompts)
    mine = kv_heads // n_row
    dims = (n_sec, n_row, n_col, units, quarter, heads_per, pairs_per, kv_heads)
    dma = pltpu.SemaphoreType.DMA
    handed, new_kv = pl.pallas_call(
        functools.partial(kernel, dims),
        out_shape=(
            jax.ShapeDtypeStruct((rows, heads_per * n_col // n_row * HEAD_DIM), BF16),
            jax.ShapeDtypeStruct((rows, 2 * cache_width), BF16),
        ),
        in_specs=[pl.BlockSpec(memory_space=pltpu.HBM)] * 6,
        out_specs=[pl.BlockSpec(memory_space=pltpu.VMEM)] * 2,
        scratch_shapes=[
            pltpu.VMEM((n_row, width, quarter * HEAD_DIM), BF16),
            pltpu.VMEM((prompts, positions, 2, cache_width), BF16),
            pltpu.VMEM((prompts, positions, cache_width), BF16),
            pltpu.VMEM((prompts, positions, cache_width), BF16),
            pltpu.VMEM((1, width), F32),
            pltpu.SMEM((1, prompts), jnp.int32),
            pltpu.VMEM((2, 2 * rows, width // 2), BF16),
            pltpu.VMEM((n_col, 2, rows, width // 2), BF16),
            pltpu.VMEM((n_col, units, rows, HEAD_DIM), BF16),
            pltpu.VMEM((n_col, n_row, quarter, rows, HEAD_DIM), BF16),
            pltpu.VMEM((n_col, quarter, rows, HEAD_DIM), BF16),
            pltpu.VMEM((n_col * units, rows, HEAD_DIM), BF16),
            pltpu.VMEM((kv_heads, prompts, tall, HEAD_DIM), BF16),
            pltpu.VMEM((n_row, mine, prompts, tall, HEAD_DIM), BF16),
            pltpu.VMEM((kv_heads, 8, tall), F32),
            pltpu.VMEM((n_row, mine, 8, tall), F32),
            pltpu.VMEM((n_row, rows, HEAD_DIM), F32),
            pltpu.VMEM((rows, heads_per * n_col // n_row * HEAD_DIM), BF16),
            dma((2 * n_row + 2,)),
            dma,
            dma((4,)),
            dma((n_col, 2)),
            dma((n_col, 2)),
            dma((2,)),
            dma((n_col, n_row)),
            dma((n_col, n_row)),
            dma((n_col,)),
            dma((n_col,)),
            dma((n_col, n_row)),
            dma((n_col, n_row)),
            dma((n_row,)),
            dma((n_row,)),
            dma((n_row,)),
            dma((n_row,)),
            dma((n_row,)),
            dma((n_row,)),
            dma((mine, prompts)),
            dma((mine, prompts)),
        ],
        compiler_params=pltpu.CompilerParams(
            collective_id=0, has_side_effects=True, vmem_limit_bytes=54912 * 1024
        ),
    )(
        hidden_in[0],
        norm_gain,
        q_weight[0],
        kv_weight[0],
        kv_cache[0],
        lengths,
    )
    return handed[None], new_kv[None]


def solution(mesh):
    n_sec, n_row, n_col = (mesh.shape[name] for name in ("section", "row", "col"))
    return jax.shard_map(
        functools.partial(shards, n_sec, n_row, n_col),
        mesh=mesh,
        in_specs=(
            P("section", "col", "row"),
            P("section", "row"),
            P("section", "row", "col"),
            P("section", "row", "col"),
            P("section", "col", "row", None, None),
            P("section", "col"),
        ),
        out_specs=(P("section", "col", "row"), P("section", "col", None)),
        check_vma=False,
    )
```
